256 devices in a mesh: dp: 64 (over y, z, core), mp: 4 (over x).
Axes of the slice: x: 4, y: 4, z: 8, core: 2. Of those that a mesh axis runs over, the one named last changes fastest.
Arguments:
- projected: bfloat16 [3, 8192, 3072], P(None, 'dp', 'mp'), may hold values from -32 to 32
- lengths: int32 [256], P('dp'), may hold values from 16 to 64, as said below
- owners: int32 [256], P('dp'), may hold values from 0 to 63, as said below
- cotangent: bfloat16 [16384, 6144], P('dp', 'mp'), may hold values from -0.125 to 0.125
Outputs:
- attended: bfloat16 [16384, 3072], P('dp', 'mp')
- out_grad: float32 [24, 128, 6144], P('mp', 'dp')
The draws below stay inside these ranges and needn't reach their ends.
Inputs may be any that keep to these rules, and one draw needn't show every extreme that they name: `lengths`: each group's 4 images fill its 128 rows exactly; every group has one image of exactly 64 patches. `owners`: an image's owner is its own group or one of the two beside it (group 0 and the last group are neighbours); a group sends at most one image to each side; in some group the image sent right has 64 patches, and in some group the image sent left has.
All inputs are finite; a program needn't handle non-finite values.
Results may differ from the reference program's by a relative error of at most 0.0062.
Values may be sent and summed in bfloat16 or wider, within the bound.
A program may use at most 128 MiB of HBM per device.

```python
import jax
import jax.numpy as jnp
from jax import lax

D = 6144
HD = 128
HEADS = 24
IMGS = 4
ROWS = 128
MAXLEN = 64
PACK = 256
IMAGES = 256
TOTAL_ROWS = 8192
N_DP = 64


def image_plan(key):
    groups = IMAGES // IMGS
    keys_all = jax.random.split(key, 8)
    base_len = ROWS // 8
    spare = ROWS // 2 - 3 * base_len
    cuts = jnp.sort(jax.random.randint(keys_all[0], (groups, 2), 0, spare + 1), axis=1)
    smaller = jnp.stack([cuts[:, 0], cuts[:, 1] - cuts[:, 0], spare - cuts[:, 1]], axis=1) + base_len
    ordered = jnp.concatenate([jnp.full((groups, 1), MAXLEN, jnp.int32), smaller.astype(jnp.int32)], axis=1)
    big_slot = jax.random.randint(keys_all[1], (groups,), 0, IMGS)
    slots = jnp.arange(IMGS, dtype=jnp.int32)
    picker = (slots[None, :] - big_slot[:, None]) % IMGS
    sizes = jnp.take_along_axis(ordered, picker, axis=1)
    group_ids = jnp.arange(groups, dtype=jnp.int32)
    first_pick = jax.random.randint(keys_all[2], (groups,), 0, IMGS)
    second_pick = (first_pick + 1 + jax.random.randint(keys_all[3], (groups,), 0, IMGS - 1)) % IMGS
    other_pick = (big_slot + 1 + jax.random.randint(keys_all[4], (groups,), 0, IMGS - 1)) % IMGS
    right_group = jax.random.randint(keys_all[5], (), 0, groups)
    left_group = (right_group + 1 + jax.random.randint(keys_all[6], (), 0, groups - 1)) % groups
    right_slot = jnp.where(group_ids == right_group, big_slot, jnp.where(group_ids == left_group, other_pick, first_pick))
    left_slot = jnp.where(group_ids == left_group, big_slot, jnp.where(group_ids == right_group, other_pick, second_pick))
    flags = jax.random.randint(keys_all[7], (groups, 2), 0, 4)
    go_right = (flags[:, 0] > 0) | (group_ids == right_group)
    go_left = (flags[:, 1] > 0) | (group_ids == left_group)
    sends_right = go_right[:, None] & (slots[None, :] == right_slot[:, None])
    sends_left = go_left[:, None] & (slots[None, :] == left_slot[:, None])
    targets = jnp.where(sends_right, group_ids[:, None] + 1, jnp.where(sends_left, group_ids[:, None] - 1, group_ids[:, None])) % groups
    return (sizes.reshape(IMAGES).astype(jnp.int32), targets.reshape(IMAGES).astype(jnp.int32))


def draw_lengths(key, part):
    return image_plan(key)[0]


def draw_owners(key, part):
    return image_plan(key)[1]


def draw_projected(key, part):
    key = jax.random.fold_in(key, 11)
    first_key, second_key = jax.random.split(key, 2)
    shape_full = (3, TOTAL_ROWS, HEADS, HD)
    base_values = jnp.clip(jax.random.normal(first_key, shape_full, jnp.float32), -4.0, 4.0)
    low_log, high_log = (-0.693, 0.693)
    scales = jnp.exp(jax.random.uniform(second_key, (3, TOTAL_ROWS, HEADS, 1), jnp.float32, low_log, high_log))
    component = jnp.array([1.0, 1.0, 4.0], jnp.float32).reshape(3, 1, 1, 1)
    return (base_values * scales * component).reshape(3, TOTAL_ROWS, HEADS * HD).astype(jnp.bfloat16)


def block_levels(key, extent, shards, smallest, high):
    def one(axis_at, shards_of):
        draws = jax.random.uniform(jax.random.fold_in(jax.random.fold_in(key, 6), axis_at), (shards_of,), jnp.float32, smallest / len(shards), high / len(shards))
        return jnp.repeat(jnp.exp(draws), extent[axis_at] // shards_of).reshape((-1,) + (1,) * (len(extent) - axis_at - 1))

    loudness = one(*shards[0])
    for cut in shards[1:]:
        loudness = loudness * one(*cut)
    return loudness


def normal_values(own_key, shape, scale, most, shards=(), kind=jnp.bfloat16):
    entries = jax.random.normal(own_key, shape, jnp.float32) * scale
    if len(shards) > 0:
        entries = block_levels(own_key, shape, shards, -0.22, 0.18) * entries
    return jnp.clip(entries, min=-most, max=most).astype(kind)


def setup_inputs(seed: int = 0) -> dict:
    key_of = jax.random.split(jax.random.key(seed), 5)
    projected = draw_projected(jax.random.fold_in(key_of[4], 71), 0)
    lengths = draw_lengths(jax.random.fold_in(key_of[4], 71), 0)
    owners = draw_owners(jax.random.fold_in(key_of[4], 71), 0)
    cotangent = normal_values(key_of[3], (PACK * N_DP, D), (TOTAL_ROWS // 4) ** -0.5, 0.125, ((0, 64), (1, 4)))
    return {"projected": projected, "lengths": lengths, "owners": owners, "cotangent": cotangent}


def norm_heads(values):
    centred = values - lax.optimization_barrier(jnp.mean(values, axis=-1, keepdims=True))
    spread = lax.optimization_barrier(jnp.mean(centred * centred, axis=-1, keepdims=True))
    return (centred * lax.rsqrt(spread + 1e-06)).astype(jnp.bfloat16)

def window_corner(sizes, starts, heading, target, span, rows):
    chosen = heading == target
    amount = jnp.sum(jnp.where(chosen, sizes, 0)).astype(jnp.int32)
    first_row = jnp.sum(jnp.where(chosen, starts, 0)).astype(jnp.int32)
    corner = jnp.minimum(first_row, rows - span).astype(jnp.int32)
    places = jnp.arange(span, dtype=jnp.int32)
    inside = (places >= first_row - corner) & (places < first_row - corner + amount)
    return (corner, inside)

def own_segments(sizes, starts, heading, rows):
    places = jnp.arange(rows, dtype=jnp.int32)
    image_of = lax.optimization_barrier(jnp.sum((places[:, None] >= (starts + sizes)[None, :]).astype(jnp.int32), axis=1)).astype(jnp.int32)
    matches = image_of[:, None] == jnp.arange(sizes.shape[0], dtype=jnp.int32)[None, :]
    staying = lax.optimization_barrier(jnp.sum(jnp.where(matches, heading[None, :], 0), axis=1)) == 0
    return jnp.where(staying, image_of, -1).astype(jnp.int32)

def attend(packed, segment):
    count = packed.shape[1]
    queries = norm_heads(packed[0].astype(jnp.float32).reshape(count, HEADS, HD))
    keys_norm = norm_heads(packed[1].astype(jnp.float32).reshape(count, HEADS, HD))
    values_all = packed[2].reshape(count, HEADS, HD)
    scores = jnp.einsum('qhd,khd->hqk', queries.astype(jnp.float32), keys_norm.astype(jnp.float32)) * HD ** (-0.5)
    allowed = (segment[:, None] == segment[None, :]) & (segment[:, None] >= 0)
    raised = jnp.where(allowed[None], jnp.exp(scores), 0.0)
    totals = lax.optimization_barrier(jnp.sum(raised, axis=-1, keepdims=True))
    weights = (raised / jnp.where((segment >= 0)[None, :, None], totals, 1.0)).astype(jnp.bfloat16)
    result = jnp.einsum('hqk,khd->qhd', weights.astype(jnp.float32), values_all.astype(jnp.float32))
    return result.astype(jnp.bfloat16).reshape(count, HEADS * HD)

def reference(projected, lengths, owners, cotangent):
    groups = IMAGES // IMGS
    width = HEADS * HD
    source = projected.reshape(3, groups, ROWS, width)
    size_table = lengths.reshape(groups, IMGS)
    owner_table = owners.reshape(groups, IMGS)
    pack_cotangent = cotangent.reshape(groups, PACK, D)

    def describe_group(group):
        sizes = size_table[group].astype(jnp.int32)
        starts = (jnp.cumsum(sizes) - sizes).astype(jnp.int32)
        heading = ((owner_table[group] - group) % groups).astype(jnp.int32)
        return (sizes, starts, heading)

    def incoming(group, target):
        sizes, starts, heading = describe_group(group)
        corner, inside = window_corner(sizes, starts, heading, target, MAXLEN, ROWS)
        block_rows = lax.dynamic_index_in_dim(source, group, 1, keepdims=False)
        return (lax.dynamic_slice_in_dim(block_rows, corner, MAXLEN, 1), inside)

    def step(running, group):
        sizes, starts, heading = describe_group(group)
        own_part = lax.dynamic_index_in_dim(source, group, 1, keepdims=False)
        from_left, inside_left = incoming(((group - 1) % groups).astype(jnp.int32), 1)
        from_right, inside_right = incoming(((group + 1) % groups).astype(jnp.int32), groups - 1)
        packed = jnp.concatenate([own_part, from_left, from_right], axis=1)
        segment = jnp.concatenate([own_segments(sizes, starts, heading, ROWS), jnp.where(inside_left, 4, -1).astype(jnp.int32), jnp.where(inside_right, 5, -1).astype(jnp.int32)]).astype(jnp.int32)
        outputs = attend(packed, segment)
        running = running + jnp.dot(outputs.T, pack_cotangent[group], preferred_element_type=jnp.float32)
        return (running, outputs)
    start_total = jnp.zeros((width, D), jnp.float32)
    grads, outputs = lax.scan(step, start_total, jnp.arange(groups, dtype=jnp.int32))
    return (outputs.reshape(groups * PACK, width), grads.reshape(HEADS, HD, D))
```

```python
import functools

import jax
import jax.numpy as jnp
from jax import lax
from jax.experimental import pallas as pl
from jax.experimental.pallas import tpu as pltpu
from jax.sharding import PartitionSpec as P

MESH = pl.DeviceIdType.MESH
BF16 = jnp.bfloat16
F32 = jnp.float32
NX, NY, NZ = 4, 4, 8
HD = 128
HEADS = 6
WIDTH = HEADS * HD
ROWS = 128
SPAN = 64
PACK = 256
IMGS = 4
GROUPS = 2 * NY * NZ
FEAT = 1536
HALF = FEAT // 2
CHUNK = 256
SHARE = 24
D = 6144
RING = {"y": NY, "z": NZ}
BLOCK = {"y": NZ * SHARE, "z": NY * SHARE}

UNITS = [
    (0, 0, "y"), (0, 1, "z"), (1, 0, "y"), (3, 0, "z"), (1, 1, "y"), (3, 1, "y"),
    (1, 2, "z"), (3, 2, "y"), (2, 0, "y"), (2, 1, "z"), (2, 2, "y"), (0, 2, "z"),
]


def place():
    dp = lax.axis_index("dp")
    chip = dp // 2
    return chip // NZ, chip % NZ, dp % 2, lax.axis_index("mp")


def device(y, z, core, x):
    return ((y % NY * NZ + z % NZ) * 2 + core, x % NX)


def plan_steps():
    ready = {("A", 0): 8.0, ("A", 1): 15.5, ("A", 3): 15.5, ("A", 2): 19.5}
    tasks = {}
    for u, (r, fu, first) in enumerate(UNITS):
        second = "z" if first == "y" else "y"
        h1, h2 = RING[first] // 2, RING[second] // 2
        size = BLOCK[first] * CHUNK * 2
        tasks[("M", u)] = ([("A", r)], 0.5, None)
        for k in range(h1):
            for s in (0, 1):
                needs = [("M", u)] + ([("R1", u, s, k - 1)] if k else [])
                sent = size // 2 if k == 0 else size
                tasks[("S1", u, s, k)] = (needs, 0.1, (("R1", u, s, k), first, s, sent))
        tasks[("F1", u)] = ([("R1", u, 0, h1 - 1), ("R1", u, 1, h1 - 1)], 0.1, None)
        for k in range(h2):
            for s in (0, 1):
                if k == 0 and s != u % 2:
                    continue
                needs = [("F1", u)]
                if k > 1 or (k == 1 and s == u % 2):
                    needs.append(("R2", u, s, k - 1))
                tasks[("S2", u, s, k)] = (needs, 0.1, (("R2", u, s, k), second, s, 12288))
        tasks[("F2", u)] = ([("R2", u, 0, h2 - 1), ("R2", u, 1, h2 - 1)], 0.1, None)
    depth = {"M": 0, "S1": 1, "F1": 6, "S2": 7, "F2": 12}

    def rank(name):
        return (name[1], -depth[name[0]] - (name[3] if len(name) > 2 else 0), name[2:])

    done = dict(ready)
    links = {}
    now = 8.0
    order = []
    while tasks:
        best = None
        for name, (needs, _, _) in tasks.items():
            if all(n in done for n in needs):
                at = max(done[n] for n in needs)
                key = (0, 0.0) if at <= now else (1, at)
                if best is None or (key, rank(name)) < best[0]:
                    best = ((key, rank(name)), name, at)
        _, name, at = best
        _, spent, message = tasks.pop(name)
        now = max(now, at) + spent
        done[name] = now
        order.append(name)
        if message:
            label, axis, s, size = message
            end = max(links.get((axis, s), 0.0), now) + size / 50e3
            links[(axis, s)] = end
            done[label] = end + 1.7
    return order


def attend(len_ref, own_ref, proj_ref, group, att):
    lens = [len_ref[j] for j in range(IMGS)]
    ends = [lens[0], lens[0] + lens[1], lens[0] + lens[1] + lens[2]]
    starts = [jnp.int32(0)] + ends
    stops = ends + [ends[2] + lens[3]]
    row = lax.broadcasted_iota(jnp.int32, (ROWS, ROWS), 0)
    col = lax.broadcasted_iota(jnp.int32, (ROWS, ROWS), 1)

    def image(at):
        return sum((at >= e).astype(jnp.int32) for e in ends)

    same = image(row) == image(col)
    scale = HD ** (-0.5)

    def norm(values):
        values = values.astype(F32)
        centred = values - jnp.mean(values, axis=-1, keepdims=True)
        spread = jnp.mean(centred * centred, axis=-1, keepdims=True)
        return (centred * lax.rsqrt(spread + 1e-06)).astype(BF16)

    for h in range(HEADS):
        lanes = slice(h * HD, (h + 1) * HD)
        q = norm(proj_ref[0, :, lanes])
        k = norm(proj_ref[1, :, lanes])
        scores = lax.dot_general(q, k, (((1,), (1,)), ((), ())), preferred_element_type=F32) * scale
        raised = jnp.where(same, jnp.exp(scores), 0.0)
        totals = jnp.sum(raised, axis=-1, keepdims=True)
        weights = (raised / totals).astype(BF16)
        out = jnp.dot(weights, proj_ref[2, :, lanes], preferred_element_type=F32)
        att[:, lanes] = out.astype(BF16)

    stays = jnp.zeros((ROWS, ROWS), jnp.bool_)
    for j in range(IMGS):
        stays = stays | ((row >= starts[j]) & (row < stops[j]) & (own_ref[j] == group))
    picks = [jnp.where((row == col) & stays, 1.0, 0.0).astype(BF16)]
    row64 = lax.broadcasted_iota(jnp.int32, (SPAN, ROWS), 0)
    col64 = lax.broadcasted_iota(jnp.int32, (SPAN, ROWS), 1)
    for step in (1, GROUPS - 1):
        target = (group + step) % GROUPS
        first = jnp.int32(0)
        stop = jnp.int32(0)
        for j in range(IMGS):
            chosen = own_ref[j] == target
            first = first + jnp.where(chosen, starts[j], 0)
            stop = stop + jnp.where(chosen, stops[j], 0)
        corner = jnp.minimum(first, ROWS - SPAN)
        pick = (col64 == row64 + corner) & (col64 >= first) & (col64 < stop)
        picks.append(jnp.where(pick, 1.0, 0.0).astype(BF16))
    return picks


def order_matrix(y, z):
    i = lax.broadcasted_iota(jnp.int32, (WIDTH, HD), 0)
    lane = lax.broadcasted_iota(jnp.int32, (WIDTH, HD), 1)
    block = (i * 2731) >> 16
    inner = i - SHARE * block
    core = (inner >= SHARE // 2).astype(jnp.int32)
    inner = inner - (SHARE // 2) * core
    yd = ((block >> 3) + y) & (NY - 1)
    zd = ((block & (NZ - 1)) + z) & (NZ - 1)
    d = ((yd * NZ + zd) * 2 + core) * 2 + (inner & 1)
    head = inner >> 1
    return [jnp.where((lane == d) & (head == h), 1.0, 0.0).astype(BF16) for h in range(HEADS)]


def kernel(
    steps, len_ref, own_ref, proj_ref, cot_ref, att_out, grad_out,
    att, outb, cotb, gathered, order, turned, partial, sum1_out, sum1_in, sum2, sum2_out, sum2_in, final, grads,
    send_sem, recv_sem, local_sem,
):
    y, z, core, x = place()
    other = 1 - core
    group = (y * NZ + z) * 2 + core
    chip = y * NZ + z
    after = (chip + 1) % (NY * NZ)
    before = (chip + NY * NZ - 1) % (NY * NZ)

    def at_chip(c, which):
        return (c * 2 + which, x)

    sibling = device(y, z, other, x)
    near = {
        ("y", 0): device(y + 1, z, core, x), ("y", 1): device(y + NY - 1, z, core, x),
        ("z", 0): device(y, z + 1, core, x), ("z", 1): device(y, z + NZ - 1, core, x),
        ("x", 0): device(y, z, core, x + 1), ("x", 1): device(y, z, core, x + NX - 1),
    }
    partners = [sibling] + list(near.values())
    partners += [at_chip(c, which) for c in (after, before) for which in (0, 1)]
    partners += [device(y, z, other, x + 1), device(y, z, other, x + NX - 1)]
    partners += [device(y, z, core, x + 2), device(y, z, other, x + 2)]
    barrier = pltpu.get_barrier_semaphore()
    for p in partners:
        pl.semaphore_signal(barrier, inc=1, device_id=p, device_id_type=MESH)

    counter = [0]
    sent = []

    def message(src, dst, target):
        n = counter[0]
        counter[0] += 1
        copy = pltpu.make_async_remote_copy(
            src_ref=src, dst_ref=dst, send_sem=send_sem.at[n], recv_sem=recv_sem.at[n],
            device_id=target, device_id_type=MESH,
        )
        copy.start()
        sent.append(copy)
        return copy

    def rows(start, size):
        return pl.ds(pl.multiple_of(start, 64), size)

    own_rows = rows(core * PACK, PACK)
    lanes = pl.ds(pl.multiple_of(core * HALF, HALF), HALF)
    lanes_other = pl.ds(pl.multiple_of(other * HALF, HALF), HALF)
    cot_here = pltpu.make_async_copy(cot_ref.at[:, lanes], cotb.at[own_rows], local_sem.at[0])
    cot_here.start()

    picks = attend(len_ref, own_ref, proj_ref, group, att)
    stay_rows = rows(core * PACK, ROWS)
    for n, pick in enumerate(picks):
        part = jnp.dot(pick, att[...], preferred_element_type=F32).astype(BF16)
        size = pick.shape[0]
        start = 0 if n == 0 else ROWS + SPAN * (n - 1)
        outb[start : start + size] = part
        if n == 0:
            gathered[0, stay_rows] = part

    pl.semaphore_wait(barrier, len(partners))

    inner_src = outb.at[rows(ROWS + SPAN * core, SPAN)]
    outer_src = outb.at[rows(ROWS + SPAN * other, SPAN)]
    inner_dst = rows((PACK + ROWS) * other + (ROWS + SPAN) * core, SPAN)
    outer_dst = rows((PACK + ROWS + SPAN) * other + ROWS * core, SPAN)
    outer_chip = before * other + after * core
    inner_here = pltpu.make_async_copy(inner_src, gathered.at[0, inner_dst], local_sem.at[1])
    inner_here.start()
    left_rows = pl.ds(ROWS, SPAN)
    right_rows = pl.ds(PACK + ROWS + SPAN, SPAN)
    outer = []
    base = counter[0]
    for which in (0, 1):
        copy = pltpu.make_async_remote_copy(
            src_ref=outer_src, dst_ref=gathered.at[0, outer_dst],
            send_sem=send_sem.at[base + which], recv_sem=recv_sem.at[base + core],
            device_id=at_chip(outer_chip, which), device_id_type=MESH,
        )
        copy.start()
        sent.append(copy)
    counter[0] += 2
    for which, place_in in ((0, right_rows), (1, left_rows)):
        outer.append(
            pltpu.make_async_remote_copy(
                src_ref=outb.at[pl.ds(0, SPAN)], dst_ref=gathered.at[0, place_in],
                send_sem=send_sem.at[base + which], recv_sem=recv_sem.at[base + which],
                device_id=sibling, device_id_type=MESH,
            )
        )
    first_half = rows(core * PACK, ROWS)
    second_half = rows(core * PACK + ROWS, ROWS)
    stay_cp = message(outb.at[pl.ds(0, ROWS)], gathered.at[0, stay_rows], sibling)
    inner_cp = message(inner_src, gathered.at[0, inner_dst], sibling)
    plus_a = message(gathered.at[0, first_half], gathered.at[3, first_half], near[("x", 0)])
    minus_a = message(gathered.at[0, first_half], gathered.at[1, first_half], near[("x", 1)])
    cot_cp = message(cot_ref.at[:, lanes_other], cotb.at[own_rows], sibling)

    for h, piece in enumerate(order_matrix(y, z)):
        order[:, h * HD : (h + 1) * HD] = piece

    inner_here.wait()
    inner_cp.wait_recv()
    for copy in outer:
        copy.wait_recv()
    plus_b = message(gathered.at[0, second_half], gathered.at[3, second_half], near[("x", 0)])
    minus_b = message(gathered.at[0, second_half], gathered.at[1, second_half], near[("x", 1)])
    stay_cp.wait_recv()

    def turn(r):
        for b in range(0, WIDTH, PACK):
            turned[r, b : b + PACK] = lax.dot_general(
                order[b : b + PACK], gathered[r], (((1,), (1,)), ((), ())), preferred_element_type=F32
            ).astype(BF16)

    turn(0)
    att_out[...] = gathered[0, own_rows]
    cot_here.wait()
    cot_cp.wait_recv()

    passed = {}

    def relay_near():
        plus_a.wait_recv()
        minus_a.wait_recv()
        relay_plus = message(gathered.at[3, first_half], gathered.at[2, first_half], near[("x", 0)])
        plus_b.wait_recv()
        minus_b.wait_recv()
        relay_minus = message(gathered.at[1, second_half], gathered.at[2, second_half], near[("x", 1)])
        passed[3] = message(gathered.at[3, own_rows], gathered.at[3, own_rows], sibling)
        passed[1] = message(gathered.at[1, own_rows], gathered.at[1, own_rows], sibling)
        passed["far"] = (relay_plus, relay_minus)

    def relay_far():
        for copy in passed["far"]:
            copy.wait_recv()
        passed[2] = message(gathered.at[2, own_rows], gathered.at[2, own_rows], sibling)

    ready = {0}
    received = {}
    slots = {}
    used = {"y": 0, "z": 0}
    for u, (r, fu, first) in enumerate(UNITS):
        slots[u] = used[first]
        used[first] += 1

    def region1(u, s, k):
        first = UNITS[u][2]
        size = BLOCK[first]
        if k == 0:
            return pl.ds(0, size // 2)
        return pl.ds(size // 2 + (k - 1) * size, size)

    def own1(u, rel):
        first = UNITS[u][2]
        if first == "y":
            return partial[u, rel * BLOCK["y"] : (rel + 1) * BLOCK["y"]]
        per = BLOCK["y"]
        return jnp.concatenate(
            [partial[u, b * per + rel * SHARE : b * per + (rel + 1) * SHARE] for b in range(NY)], axis=0
        )

    def do_multiply(u):
        r, fu, _ = UNITS[u]
        if r not in ready:
            if r == 2:
                passed[2].wait_recv()
            else:
                passed[r].wait_recv()
            turn(r)
            ready.add(r)
        partial[u] = jnp.dot(
            turned[r], cotb[:, fu * CHUNK : (fu + 1) * CHUNK], preferred_element_type=F32
        )

    def do_first(u, s, k):
        first = UNITS[u][2]
        n = RING[first]
        far = n // 2 - k
        rel = far if s == 0 else (n - far) % n
        mine = own1(u, rel)
        size = BLOCK[first]
        out = sum1_out[first].at[slots[u], s, region1(u, s, k)]
        if k == 0:
            half = size // 2
            out[...] = mine[s * half : (s + 1) * half].astype(BF16)
        else:
            received[(1, u, s, k - 1)].wait_recv()
            got = sum1_in[first][slots[u], s, region1(u, s, k - 1)].astype(F32)
            if k == 1:
                half = size // 2
                parts = [mine[:half], mine[half:]]
                parts[s] = parts[s] + got
                total = jnp.concatenate(parts, axis=0)
            else:
                total = mine + got
            out[...] = total.astype(BF16)
        received[(1, u, s, k)] = message(out, sum1_in[first].at[slots[u], s, region1(u, s, k)], near[(first, s)])

    def do_turn(u):
        first, n2 = UNITS[u][2], RING["z" if UNITS[u][2] == "y" else "y"]
        k = RING[first] // 2 - 1
        total = own1(u, 0)
        for s in (0, 1):
            received[(1, u, s, k)].wait_recv()
            total = total + sum1_in[first][slots[u], s, region1(u, s, k)].astype(F32)
        for b in range(n2):
            block = total[b * SHARE : (b + 1) * SHARE]
            sum2[u, b] = jnp.concatenate([block[:, :HD], block[:, HD:]], axis=0)

    def do_second(u, s, k):
        second = "z" if UNITS[u][2] == "y" else "y"
        n = RING[second]
        far = n // 2 - k
        rel = far if s == 0 else (n - far) % n
        total = sum2[u, rel]
        if (2, u, s, k - 1) in received:
            received[(2, u, s, k - 1)].wait_recv()
            total = total + sum2_in[u, s, k - 1].astype(F32)
        sum2_out[u, s, k] = total.astype(BF16)
        received[(2, u, s, k)] = message(sum2_out.at[u, s, k], sum2_in.at[u, s, k], near[(second, s)])

    arriving = []

    def do_last(u):
        r, fu, first = UNITS[u]
        k = RING["z" if first == "y" else "y"] // 2 - 1
        total = sum2[u, 0]
        for s in (0, 1):
            received[(2, u, s, k)].wait_recv()
            total = total + sum2_in[u, s, k].astype(F32)
        part = SHARE // 2
        for c in (0, 1):
            for side in (0, 1):
                start = side * SHARE + c * part
                final[u, c, 0:part, side * HD : (side + 1) * HD] = total[start : start + part]
        here = pl.ds(pl.multiple_of(x * FEAT + core * HALF + fu * CHUNK, CHUNK), CHUNK)
        if r == 0:
            copy = pltpu.make_async_copy(final.at[u, core], grads.at[:, here], local_sem.at[2 + fu])
            copy.start()
            arriving.append((copy, True))
        else:
            arriving.append((message(final.at[u, core], grads.at[:, here], device(y, z, core, x + r)), False))
        arriving.append((message(final.at[u, other], grads.at[:, here], device(y, z, other, x + r)), False))

    near_done = far_done = False
    for name in steps:
        kind, u = name[0], name[1]
        if not near_done and kind == "M" and UNITS[u][0] != 0:
            relay_near()
            near_done = True
        if not far_done and kind == "M" and UNITS[u][0] == 2:
            relay_far()
            far_done = True
        if kind == "M":
            do_multiply(u)
        elif kind == "S1":
            do_first(*name[1:])
        elif kind == "F1":
            do_turn(u)
        elif kind == "S2":
            do_second(*name[1:])
        else:
            do_last(u)

    for copy, local in arriving:
        if local:
            copy.wait()
        else:
            copy.wait_recv()
    grad_out[...] = grads[0 : SHARE // 2]
    for copy in sent:
        copy.wait_send()


def shards(projected, lengths, owners, cotangent):
    steps = plan_steps()
    units = len(UNITS)
    counts = {a: sum(1 for unit in UNITS if unit[2] == a) for a in ("y", "z")}
    lead = {a: BLOCK[a] // 2 + (RING[a] // 2 - 1) * BLOCK[a] for a in ("y", "z")}
    messages = 160
    sums = {a: pltpu.VMEM((counts[a], 2, lead[a], CHUNK), BF16) for a in ("y", "z")}
    vmem = pl.BlockSpec(memory_space=pltpu.VMEM)
    smem = pl.BlockSpec(memory_space=pltpu.SMEM)
    scratch = [
        pltpu.VMEM((ROWS, WIDTH), BF16),
        pltpu.VMEM((PACK, WIDTH), BF16),
        pltpu.VMEM((2 * PACK, HALF), BF16),
        pltpu.VMEM((NX, 2 * PACK, WIDTH), BF16),
        pltpu.VMEM((WIDTH, WIDTH), BF16),
        pltpu.VMEM((NX, WIDTH, 2 * PACK), BF16),
        pltpu.VMEM((units, WIDTH, CHUNK), F32),
        sums,
        sums,
        pltpu.VMEM((units, NZ, 2 * SHARE, HD), F32),
        pltpu.VMEM((units, 2, NZ // 2, 2 * SHARE, HD), BF16),
        pltpu.VMEM((units, 2, NZ // 2, 2 * SHARE, HD), BF16),
        pltpu.VMEM((units, 2, 16, CHUNK), F32),
        pltpu.VMEM((16, D), F32),
        pltpu.SemaphoreType.DMA((messages + 40,)),
        pltpu.SemaphoreType.DMA((messages + 40,)),
        pltpu.SemaphoreType.DMA((8,)),
    ]
    attended, grads = pl.pallas_call(
        functools.partial(kernel, steps),
        out_shape=(
            jax.ShapeDtypeStruct((PACK, WIDTH), BF16),
            jax.ShapeDtypeStruct((SHARE // 2, D), F32),
        ),
        in_specs=[smem, smem, vmem, pl.BlockSpec(memory_space=pl.ANY)],
        out_specs=(vmem, vmem),
        scratch_shapes=scratch,
        compiler_params=pltpu.CompilerParams(
            collective_id=0, has_side_effects=True, vmem_limit_bytes=56 * 2**20
        ),
        name="attend_and_reduce",
    )(lengths, owners, projected, cotangent)
    return attended, grads.reshape(HEADS, 2, D)


def solution(mesh):
    return jax.shard_map(
        shards,
        mesh=mesh,
        in_specs=(P(None, "dp", "mp"), P("dp"), P("dp"), P("dp", "mp")),
        out_specs=(P("dp", "mp"), P("mp", "dp", None)),
        check_vma=False,
    )
```

```python
import functools

import jax
import jax.numpy as jnp
from jax import lax
from jax.experimental import pallas as pl
from jax.experimental.pallas import tpu as pltpu
from jax.sharding import PartitionSpec as P

MESH = pl.DeviceIdType.MESH
BF16 = jnp.bfloat16
F32 = jnp.float32
NX, NY, NZ = 4, 4, 8
HD = 128
HEADS = 6
PART = HEADS // 2
WIDTH = HEADS * HD
HALF = PART * HD
ROWS = 128
SPAN = 64
PACK = 256
IMGS = 4
GROUPS = 2 * NY * NZ
FEAT = 1536
CHUNK = 512
SHARE = 2 * PART * 2
STACK = SHARE * CHUNK // HD
D = 6144
RING = {"y": NY, "z": NZ}
BLOCK = {"y": NZ * SHARE, "z": NY * SHARE}
OTHER = {"y": "z", "z": "y"}

UNITS = [
    (0, 0, "y", 0), (0, 1, "z", 0), (0, 2, "y", 0), (1, 0, "y", 0), (3, 0, "z", 0), (1, 1, "y", 0),
    (3, 1, "z", 0), (1, 2, "y", 1), (3, 2, "z", 1), (2, 0, "y", 1), (2, 1, "y", 1), (2, 2, "y", 1),
]


def place():
    dp = lax.axis_index("dp")
    chip = dp // 2
    return chip // NZ, chip % NZ, dp % 2, lax.axis_index("mp")


def device(y, z, core, x):
    return ((y % NY * NZ + z % NZ) * 2 + core, x % NX)


def second_routes(u, units):
    _, _, first, direct = units[u]
    n = RING[OTHER[first]]
    routes = []
    if direct:
        for rel in sorted(range(1, n), key=lambda v: -min(v, n - v)):
            routes.append((rel, 0 if rel <= n // 2 else 1, min(rel, n - rel), rel, None))
        return routes, [route[0] for route in routes]
    for k in range(n // 2):
        for s in (0, 1):
            if k == 0 and s != u % 2:
                continue
            far = n // 2 - k
            adds = s * 4 + k - 1 if k > 1 or (k == 1 and s == u % 2) else None
            routes.append((s * 4 + k, s, 1, far if s == 0 else (n - far) % n, adds))
    return routes, [n // 2 - 1, 4 + n // 2 - 1]


def plan_steps(units, weights=(1.0, 0.0), detail=False):
    start = 9.5
    lat, hop, rate = 2.6, 0.6, 46e3
    done = {"B": start}
    links = {}
    tasks = {}

    def put(name, needs, spent, out=None):
        tasks[name] = (needs, spent, out)

    put(("X", 0), ["B"], 0.3, [
        ("outer", "z0", 1, 98304), ("p0", "x0", 1, 147456), ("p1", "x0", 1, 147456),
        ("m0", "x1", 1, 147456), ("m1", "x1", 1, 147456),
    ])
    put(("X", 1), ["outer"], 0.1, [("po", "x0", 1, 98304), ("mo", "x1", 1, 98304)])
    put(("X", 2), ["p0"], 0.1, [("f0", "x0", 1, 147456)])
    put(("X", 3), ["m1"], 0.1, [("f1", "x1", 1, 147456)])
    put(("X", 4), ["po", "mo", ("X", 2), ("X", 3)], 0.1, [("f2", "x0", 1, 49152), ("f3", "x1", 1, 49152)])
    feeds = {0: [("X", 1)], 1: ["m0", "m1", "mo"], 3: ["p0", "p1", "po"], 2: ["f0", "f1", "f2", "f3"]}
    for u, (r, fu, first, direct) in enumerate(units):
        h1, h2 = RING[first] // 2, RING[OTHER[first]] // 2
        size = BLOCK[first] * CHUNK * 2
        put(("M", u), feeds[r], 0.35)
        for k in range(h1):
            for s in (0, 1):
                needs = [("M", u)] + ([("R1", u, s, k - 1)] if k else [])
                sent = size // 2 if k == 0 else size
                put(("S1", u, s, k), needs, 0.1, [(("R1", u, s, k), first + str(s), 1, sent)])
        put(("F1", u), [("R1", u, 0, h1 - 1), ("R1", u, 1, h1 - 1)], 0.15)
        routes, ends = second_routes(u, units)
        for key, s, hops, _, adds in routes:
            needs = [("F1", u)] + ([("R2", u, adds)] if adds is not None else [])
            put(("S2", u, key), needs, 0.07, [(("R2", u, key), OTHER[first] + str(s), hops, 12288)])
        put(("F2", u), [("R2", u, key) for key in ends], 0.1, [(("O", u), "o", 1 + (r == 2), 32768)])
    depth = {"M": 0, "S1": 1, "F1": 6, "S2": 7, "F2": 12, "X": 50}

    def rank(name):
        level = depth[name[0]]
        if name[0] == "S1":
            level += name[3]
        if name[0] == "X":
            return (-100.0, name[1])
        return (weights[0] * name[1] + weights[1] * level, name[1], -level, name[2:])

    now = start
    order = []
    while tasks:
        best = None
        for name, (needs, _, _) in tasks.items():
            if all(n in done for n in needs):
                at = max(done[n] for n in needs)
                key = (0, 0.0) if at <= now else (1, at)
                if best is None or (key, rank(name)) < best[0]:
                    best = ((key, rank(name)), name, at)
        _, name, at = best
        _, spent, out = tasks.pop(name)
        now = max(now, at) + spent
        done[name] = now
        order.append(name)
        for label, link, hops, size in out or []:
            end = max(links.get(link, 0.0), now) + hops * size / rate
            links[link] = end
            done[label] = end + lat + hop * (hops - 1)
    if detail:
        return order, max(done.values()), done, links
    return order


def attend(len_ref, own_ref, proj_ref, group, core, att):
    lens = [len_ref[j] for j in range(IMGS)]
    ends = [lens[0], lens[0] + lens[1], lens[0] + lens[1] + lens[2]]
    starts = [jnp.int32(0)] + ends
    stops = ends + [ends[2] + lens[3]]
    row = lax.broadcasted_iota(jnp.int32, (ROWS, ROWS), 0)
    col = lax.broadcasted_iota(jnp.int32, (ROWS, ROWS), 1)

    def image(at):
        return sum((at >= e).astype(jnp.int32) for e in ends)

    same = image(row) == image(col)
    scale = HD ** (-0.5)

    def norm(values):
        values = values.astype(F32)
        centred = values - jnp.mean(values, axis=-1, keepdims=True)
        spread = jnp.mean(centred * centred, axis=-1, keepdims=True)
        return (centred * lax.rsqrt(spread + 1e-06)).astype(BF16)

    for h in range(HEADS):
        lanes = slice(h * HD, (h + 1) * HD)
        q = norm(proj_ref[0, :, lanes])
        k = norm(proj_ref[1, :, lanes])
        scores = lax.dot_general(q, k, (((1,), (1,)), ((), ())), preferred_element_type=F32) * scale
        raised = jnp.where(same, jnp.exp(scores), 0.0)
        totals = jnp.sum(raised, axis=-1, keepdims=True)
        weights = (raised / totals).astype(BF16)
        out = jnp.dot(weights, proj_ref[2, :, lanes], preferred_element_type=F32)
        att[:, lanes] = out.astype(BF16)

    stays = jnp.zeros((ROWS, ROWS), jnp.bool_)
    for j in range(IMGS):
        stays = stays | ((row >= starts[j]) & (row < stops[j]) & (own_ref[j] == group))
    picks = [jnp.where((row == col) & stays, 1.0, 0.0).astype(BF16)]
    row64 = lax.broadcasted_iota(jnp.int32, (SPAN, ROWS), 0)
    col64 = lax.broadcasted_iota(jnp.int32, (SPAN, ROWS), 1)
    for target in (group + 1 - 2 * core, group + GROUPS - 1 + 2 * core):
        first = jnp.int32(0)
        stop = jnp.int32(0)
        for j in range(IMGS):
            chosen = own_ref[j] == target % GROUPS
            first = first + jnp.where(chosen, starts[j], 0)
            stop = stop + jnp.where(chosen, stops[j], 0)
        corner = jnp.minimum(first, ROWS - SPAN)
        pick = (col64 == row64 + corner) & (col64 >= first) & (col64 < stop)
        picks.append(jnp.where(pick, 1.0, 0.0).astype(BF16))
    return picks


def order_matrix(y, z, first):
    i = lax.broadcasted_iota(jnp.int32, (HALF, HD), 0)
    lane = lax.broadcasted_iota(jnp.int32, (HALF, HD), 1)
    block = (i * 5462) >> 16
    inner = i - SHARE * block
    core = (inner >= SHARE // 2).astype(jnp.int32)
    inner = inner - (SHARE // 2) * core
    if first == "y":
        yd, zd = block >> 3, block
    else:
        yd, zd = block, block >> 2
    yd = (yd + y) & (NY - 1)
    zd = (zd + z) & (NZ - 1)
    d = ((yd * NZ + zd) * 2 + core) * 2 + (inner & 1)
    head = inner >> 1
    return [jnp.where((lane == d) & (head == h), 1.0, 0.0).astype(BF16) for h in range(PART)]


def kernel(
    steps, len_ref, own_ref, proj_ref, cot_ref, att_out, grad_out,
    att, outb, extra, cotb, gathered, order, turned, partial, sum1_out, sum1_in, sum2, sum2_out, sum2_in, final, grads,
    send_sem, recv_sem, local_sem,
):
    y, z, core, x = place()
    other = 1 - core
    chip = y * NZ + z
    group = chip * 2 + core
    after = (chip + 1) % (NY * NZ)
    before = (chip + NY * NZ - 1) % (NY * NZ)
    sibling = device(y, z, other, x)

    def shifted(axis, by, which=None):
        c = core if which is None else which
        if axis == "x":
            return device(y, z, c, x + by % NX)
        if axis == "y":
            return device(y + by % NY, z, c, x)
        return device(y, z + by % NZ, c, x)

    partners = [sibling]
    partners += [shifted("y", by) for by in range(1, NY)]
    partners += [shifted("z", by) for by in range(1, NZ)]
    partners += [shifted("x", by, which) for by in range(1, NX) for which in (0, 1)]
    partners += [(c * 2 + which, x) for c in (after, before) for which in (0, 1)]
    barrier = pltpu.get_barrier_semaphore()
    for p in partners:
        pl.semaphore_signal(barrier, inc=1, device_id=p, device_id_type=MESH)

    counter = [0]
    sent = []

    def message(src, dst, target):
        n = counter[0]
        counter[0] += 1
        copy = pltpu.make_async_remote_copy(
            src_ref=src, dst_ref=dst, send_sem=send_sem.at[n], recv_sem=recv_sem.at[n],
            device_id=target, device_id_type=MESH,
        )
        copy.start()
        sent.append(copy)
        return copy

    def rows(start, size):
        return pl.ds(pl.multiple_of(start, 64), size)

    mine = ROWS + SPAN
    own_rows = rows(core * mine, mine)
    outer_at = 2 * mine
    cot_pieces = [
        (pl.ds(0, ROWS), rows(core * mine, ROWS)),
        (pl.ds(ROWS, SPAN), rows(other * outer_at + core * ROWS, SPAN)),
        (pl.ds(ROWS + SPAN, SPAN), rows(other * (mine + ROWS) + core * (outer_at + SPAN), SPAN)),
    ]
    cot_here = []
    for n, (src, dst) in enumerate(cot_pieces):
        copy = pltpu.make_async_copy(cot_ref.at[src], cotb.at[dst], local_sem.at[n])
        copy.start()
        cot_here.append(copy)

    picks = attend(len_ref, own_ref, proj_ref, group, core, att)
    start = 0
    for pick in picks:
        part = jnp.dot(pick, att[...], preferred_element_type=F32).astype(BF16)
        for c in (0, 1):
            outb[c, start : start + pick.shape[0]] = part[:, c * HALF : (c + 1) * HALF]
        start += pick.shape[0]
    gathered[0, own_rows] = outb[core, 0:mine]
    for n, first in enumerate(("y", "z")):
        for h, piece in enumerate(order_matrix(y, z, first)):
            order[n, :, h * HD : (h + 1) * HD] = piece

    pl.semaphore_wait(barrier, len(partners))

    outer_chip = before * other + after * core
    outer_rows = [pl.ds(outer_at, SPAN), pl.ds(outer_at + SPAN, SPAN)]
    base = counter[0]
    counter[0] += 2
    outer_dst = rows(outer_at + SPAN * other, SPAN)
    for which in (0, 1):
        copy = pltpu.make_async_remote_copy(
            src_ref=outb.at[which, pl.ds(mine, SPAN)], dst_ref=gathered.at[0, outer_dst],
            send_sem=send_sem.at[base + which], recv_sem=recv_sem.at[base + core],
            device_id=(outer_chip * 2 + which, x), device_id_type=MESH,
        )
        copy.start()
        sent.append(copy)
    outer = [
        pltpu.make_async_remote_copy(
            src_ref=outb.at[0, pl.ds(mine, SPAN)], dst_ref=gathered.at[0, outer_rows[1 - which]],
            send_sem=send_sem.at[base + which], recv_sem=recv_sem.at[base + which],
            device_id=sibling, device_id_type=MESH,
        )
        for which in (0, 1)
    ]
    inner_cp = message(outb.at[other, pl.ds(0, mine)], gathered.at[0, own_rows], sibling)
    across = {}
    for slot, by in ((3, 1), (1, 3)):
        base = counter[0]
        counter[0] += 2
        for which in (0, 1):
            copy = pltpu.make_async_remote_copy(
                src_ref=outb.at[which, pl.ds(0, mine)], dst_ref=gathered.at[slot, own_rows],
                send_sem=send_sem.at[base + which], recv_sem=recv_sem.at[base + core],
                device_id=shifted("x", by, which), device_id_type=MESH,
            )
            copy.start()
            sent.append(copy)
            across[slot, which] = pltpu.make_async_remote_copy(
                src_ref=outb.at[0, pl.ds(0, mine)], dst_ref=gathered.at[slot, pl.ds(which * mine, mine)],
                send_sem=send_sem.at[base + which], recv_sem=recv_sem.at[base + which],
                device_id=sibling, device_id_type=MESH,
            )
    cot_there = [message(cot_ref.at[src], cotb.at[dst], sibling) for src, dst in cot_pieces]
    extra_inner = message(outb.at[core, pl.ds(ROWS, SPAN)], extra.at[0], sibling)

    waited = set()

    def arrived(copy):
        if id(copy) not in waited:
            waited.add(id(copy))
            copy.wait_recv()

    moved = {}

    def do_move(n):
        if n == 0:
            return
        if n == 1:
            for copy in outer:
                arrived(copy)
            both = pl.ds(outer_at, 2 * SPAN)
            moved["po"] = message(gathered.at[0, both], gathered.at[3, both], shifted("x", 1))
            moved["mo"] = message(gathered.at[0, both], gathered.at[1, both], shifted("x", 3))
            arrived(inner_cp)
            theirs = rows(outer_at + SPAN * other, SPAN)
            moved["extra"] = message(gathered.at[0, theirs], extra.at[1], sibling)
        elif n == 2:
            arrived(across[3, 0])
            part = pl.ds(0, mine)
            moved["f0"] = message(gathered.at[3, part], gathered.at[2, part], shifted("x", 1))
        elif n == 3:
            arrived(across[1, 1])
            part = pl.ds(mine, mine)
            moved["f1"] = message(gathered.at[1, part], gathered.at[2, part], shifted("x", 3))
        else:
            arrived(moved["po"])
            arrived(moved["mo"])
            moved["f2"] = message(gathered.at[3, outer_rows[0]], gathered.at[2, outer_rows[0]], shifted("x", 1))
            moved["f3"] = message(gathered.at[1, outer_rows[1]], gathered.at[2, outer_rows[1]], shifted("x", 3))

    turned_at = {}

    def turn(r, first):
        if (r, first) in turned_at:
            return turned_at[r, first]
        if r == 2:
            for label in ("f0", "f1", "f2", "f3"):
                arrived(moved[label])
        elif r:
            arrived(across[r, 0])
            arrived(across[r, 1])
            arrived(moved["po" if r == 3 else "mo"])
        n = len(turned_at)
        turned[n] = lax.dot_general(
            order["yz".index(first)], gathered[r], (((1,), (1,)), ((), ())), preferred_element_type=F32
        ).astype(BF16)
        turned_at[r, first] = n
        return n

    def do_multiply(u):
        r, fu, first, _ = UNITS[u]
        n = turn(r, first)
        if u == 0:
            for copy in cot_here:
                copy.wait()
            for copy in cot_there:
                arrived(copy)
        partial[u] = jnp.dot(turned[n], cotb[:, fu * CHUNK : (fu + 1) * CHUNK], preferred_element_type=F32)

    received = {}

    def do_first(u, s, k):
        first = UNITS[u][2]
        n, size = RING[first], BLOCK[first]
        far = n // 2 - k
        rel = far if s == 0 else (n - far) % n
        total = partial[u, rel * size : (rel + 1) * size]
        half = pl.ds(s * CHUNK // 2, CHUNK // 2) if k == 0 else pl.ds(0, CHUNK)
        spot = (u, s, pl.ds(k * size, size), half)
        if k == 0:
            total = total[:, s * CHUNK // 2 : (s + 1) * CHUNK // 2]
        else:
            received[1, u, s, k - 1].wait_recv()
            before_rows = pl.ds((k - 1) * size, size)
            if k == 1:
                got = sum1_in[u, s, before_rows, s * CHUNK // 2 : (s + 1) * CHUNK // 2].astype(F32)
                parts = [total[:, : CHUNK // 2], total[:, CHUNK // 2 :]]
                parts[s] = parts[s] + got
                total = jnp.concatenate(parts, axis=1)
            else:
                total = total + sum1_in[u, s, before_rows].astype(F32)
        sum1_out[spot] = total.astype(BF16)
        received[1, u, s, k] = message(
            sum1_out.at[spot], sum1_in.at[spot], shifted(first, 1 if s == 0 else n - 1)
        )

    def do_turn(u):
        first = UNITS[u][2]
        size, k = BLOCK[first], RING[first] // 2 - 1
        total = partial[u, 0:size]
        for s in (0, 1):
            received[1, u, s, k].wait_recv()
            total = total + sum1_in[u, s, pl.ds(k * size, size)].astype(F32)
        for b in range(RING[OTHER[first]]):
            block = total[b * SHARE : (b + 1) * SHARE]
            sum2[u, b] = jnp.concatenate([block[:, p * HD : (p + 1) * HD] for p in range(CHUNK // HD)], axis=0)

    def do_second(u, key):
        axis = OTHER[UNITS[u][2]]
        n = RING[axis]
        _, s, hops, rel, adds = next(route for route in second_routes(u, UNITS)[0] if route[0] == key)
        total = sum2[u, rel]
        if adds is not None:
            received[2, u, adds].wait_recv()
            total = total + sum2_in[u, adds].astype(F32)
        sum2_out[u, key] = total.astype(BF16)
        received[2, u, key] = message(
            sum2_out.at[u, key], sum2_in.at[u, key], shifted(axis, hops if s == 0 else n - hops)
        )

    arriving = []

    def do_last(u):
        r, fu, _, _ = UNITS[u]
        total = sum2[u, 0]
        for key in second_routes(u, UNITS)[1]:
            received[2, u, key].wait_recv()
            total = total + sum2_in[u, key].astype(F32)
        part = SHARE // 2
        for c in (0, 1):
            for p in range(CHUNK // HD):
                start = p * SHARE + c * part
                final[u, c, 0:part, p * HD : (p + 1) * HD] = total[start : start + part]
        here = pl.ds(pl.multiple_of(x * FEAT + fu * CHUNK, CHUNK), CHUNK)
        if r == 0:
            copy = pltpu.make_async_copy(final.at[u, core], grads.at[core, :, here], local_sem.at[3 + fu])
            copy.start()
            arriving.append((copy, True))
            arriving.append((message(final.at[u, other], grads.at[core, :, here], sibling), False))
            return
        base = counter[0]
        counter[0] += 2
        for which in (0, 1):
            copy = pltpu.make_async_remote_copy(
                src_ref=final.at[u, which], dst_ref=grads.at[core, :, here],
                send_sem=send_sem.at[base + which], recv_sem=recv_sem.at[base + core],
                device_id=shifted("x", r, which), device_id_type=MESH,
            )
            copy.start()
            sent.append(copy)
            there = pl.ds(pl.multiple_of((x + NX - r) % NX * FEAT + fu * CHUNK, CHUNK), CHUNK)
            wait = pltpu.make_async_remote_copy(
                src_ref=final.at[u, which], dst_ref=grads.at[which, :, there],
                send_sem=send_sem.at[base + which], recv_sem=recv_sem.at[base + which],
                device_id=sibling, device_id_type=MESH,
            )
            arriving.append((wait, False))

    run = {"X": do_move, "M": do_multiply, "S1": do_first, "F1": do_turn, "S2": do_second, "F2": do_last}
    for name in steps:
        run[name[0]](*name[1:])

    arrived(extra_inner)
    arrived(moved["extra"])
    att_out[0:ROWS, 0:HALF] = outb[0, 0:ROWS]
    att_out[0:ROWS, HALF:WIDTH] = outb[1, 0:ROWS]
    lanes = pl.ds(pl.multiple_of(core * HALF, HD), HALF)
    lanes_other = pl.ds(pl.multiple_of(other * HALF, HD), HALF)
    from_inner = rows(ROWS + SPAN * other, SPAN)
    from_outer = rows(ROWS + SPAN * core, SPAN)
    att_out[from_inner, lanes] = gathered[0, rows(other * mine + ROWS, SPAN)]
    att_out[from_inner, lanes_other] = extra[0]
    att_out[from_outer, lanes] = gathered[0, rows(outer_at + SPAN * core, SPAN)]
    att_out[from_outer, lanes_other] = extra[1]

    for copy, local in arriving:
        if local:
            copy.wait()
        else:
            copy.wait_recv()
    for h in range(HEADS):
        row = h % PART * 2
        grad_out[h] = grads[h // PART, row : row + 2]
    for copy in sent:
        copy.wait_send()


def shards(projected, lengths, owners, cotangent):
    steps = plan_steps(UNITS)
    units = len(UNITS)
    messages = 24 + 15 * units
    vmem = pl.BlockSpec(memory_space=pltpu.VMEM)
    smem = pl.BlockSpec(memory_space=pltpu.SMEM)
    scratch = [
        pltpu.VMEM((ROWS, WIDTH), BF16),
        pltpu.VMEM((2, PACK, HALF), BF16),
        pltpu.VMEM((2, SPAN, HALF), BF16),
        pltpu.VMEM((2 * PACK, FEAT), BF16),
        pltpu.VMEM((NX, 2 * PACK, HALF), BF16),
        pltpu.VMEM((2, HALF, HALF), BF16),
        pltpu.VMEM((2 * NX, HALF, 2 * PACK), BF16),
        pltpu.VMEM((units, HALF, CHUNK), F32),
        pltpu.VMEM((units, 2, HALF // 2, CHUNK), BF16),
        pltpu.VMEM((units, 2, HALF // 2, CHUNK), BF16),
        pltpu.VMEM((units, NZ, STACK, HD), F32),
        pltpu.VMEM((units, NZ, STACK, HD), BF16),
        pltpu.VMEM((units, NZ, STACK, HD), BF16),
        pltpu.VMEM((units, 2, 8, CHUNK), F32),
        pltpu.VMEM((2, 8, D), F32),
        pltpu.SemaphoreType.DMA((messages,)),
        pltpu.SemaphoreType.DMA((messages,)),
        pltpu.SemaphoreType.DMA((8,)),
    ]
    return pl.pallas_call(
        functools.partial(kernel, steps),
        out_shape=(
            jax.ShapeDtypeStruct((PACK, WIDTH), BF16),
            jax.ShapeDtypeStruct((HEADS, 2, D), F32),
        ),
        in_specs=[smem, smem, vmem, pl.BlockSpec(memory_space=pl.ANY)],
        out_specs=(vmem, vmem),
        scratch_shapes=scratch,
        compiler_params=pltpu.CompilerParams(
            collective_id=0, has_side_effects=True, vmem_limit_bytes=56 * 2**20
        ),
        name="attend_and_reduce",
    )(lengths, owners, projected, cotangent)


def solution(mesh):
    return jax.shard_map(
        shards,
        mesh=mesh,
        in_specs=(P(None, "dp", "mp"), P("dp"), P("dp"), P("dp", "mp")),
        out_specs=(P("dp", "mp"), P("mp", "dp", None)),
        check_vma=False,
    )
```

```python
import functools

import jax
import jax.numpy as jnp
from jax import lax
from jax.experimental import pallas as pl
from jax.experimental.pallas import tpu as pltpu
from jax.sharding import PartitionSpec as P

MESH = pl.DeviceIdType.MESH
BF16 = jnp.bfloat16
F32 = jnp.float32
NX, NY, NZ = 4, 4, 8
HD = 128
HEADS = 6
PART = HEADS // 2
WIDTH = HEADS * HD
HALF = PART * HD
ROWS = 128
SPAN = 64
PACK = 256
IMGS = 4
GROUPS = 2 * NY * NZ
FEAT = 1536
SHARE = 2 * 2
STACK = SHARE * FEAT // HD
D = 6144
RING = {"y": NY, "z": NZ}
BLOCK = {"y": NZ * SHARE, "z": NY * SHARE}
OTHER = {"y": "z", "z": "y"}

UNITS = [
    (0, 0, "y", 0), (0, 1, "z", 1), (0, 2, "y", 0), (1, 0, "y", 0), (3, 0, "z", 1), (1, 1, "y", 0),
    (3, 1, "z", 1), (1, 2, "y", 1), (3, 2, "z", 1), (2, 0, "y", 1), (2, 1, "y", 1), (2, 2, "y", 1),
]
EARLY = 2
SENDING = 64


def place():
    dp = lax.axis_index("dp")
    chip = dp // 2
    return chip // NZ, chip % NZ, dp % 2, lax.axis_index("mp")


def device(y, z, core, x):
    return ((y % NY * NZ + z % NZ) * 2 + core, x % NX)


def second_routes(u, units):
    _, _, first, direct = units[u]
    n = RING[OTHER[first]]
    routes = []
    if direct:
        for rel in sorted(range(1, n), key=lambda v: -min(v, n - v)):
            routes.append((rel, 0 if rel <= n // 2 else 1, min(rel, n - rel), rel, None))
        return routes, [route[0] for route in routes]
    for k in range(n // 2):
        for s in (0, 1):
            if k == 0 and s != u % 2:
                continue
            far = n // 2 - k
            adds = s * 4 + k - 1 if k > 1 or (k == 1 and s == u % 2) else None
            routes.append((s * 4 + k, s, 1, far if s == 0 else (n - far) % n, adds))
    return routes, [n // 2 - 1, 4 + n // 2 - 1]


def plan_steps(units, weights=(1.0, 0.0), detail=False):
    start = 9.5
    lat, hop, rate = 2.6, 0.6, 46e3
    done = {"B": start}
    links = {}
    tasks = {}

    def put(name, needs, spent, out=None):
        tasks[name] = (needs, spent, out)

    early, late = 49152 * EARLY, 49152 * (PART - EARLY)
    put(("X", 0), ["B"], 0.3, [
        ("outer", "z0", 1, 49152), ("p0", "x0", 1, early), ("p1", "x0", 1, early),
        ("m0", "x1", 1, early), ("m1", "x1", 1, early),
    ])
    put(("X", 1), ["outer"], 0.2, [
        ("po", "x0", 1, 98304), ("mo", "x1", 1, 98304), ("p2", "x0", 1, late), ("p3", "x0", 1, late),
        ("m2", "x1", 1, late), ("m3", "x1", 1, late),
    ])
    put(("X", 2), ["p0"], 0.1, [("f0", "x0", 1, early)])
    put(("X", 3), ["m1"], 0.1, [("f1", "x1", 1, early)])
    put(("X", 4), ["po", "mo", ("X", 2), ("X", 3)], 0.1, [("f2", "x0", 1, 49152), ("f3", "x1", 1, 49152)])
    put(("X", 6), ["f0"], 0.2, None)
    put(("X", 5), ["p2", "m3", ("X", 4)], 0.1, [("f4", "x0", 1, late), ("f5", "x1", 1, late)])
    feeds = {0: [("X", 1)], 1: ["m0", "m1", "mo"], 3: ["p0", "p1", "po"], 2: ["f0", "f1", "f2", "f3"]}
    rest = {0: [], 1: ["m2", "m3"], 3: ["p2", "p3"], 2: ["f4", "f5"]}
    for u, (r, h, first, direct) in enumerate(units):
        h1, h2 = RING[first] // 2, RING[OTHER[first]] // 2
        size = BLOCK[first] * FEAT * 2
        put(("M", u), feeds[r] + (rest[r] if h >= EARLY else []), 0.45)
        for k in range(h1):
            for s in (0, 1):
                needs = [("M", u)] + ([("R1", u, s, k - 1)] if k else [])
                sent = size // 2 if k == 0 else size
                put(("S1", u, s, k), needs, 0.1, [(("R1", u, s, k), first + str(s), 1, sent)])
        put(("F1", u), [("R1", u, 0, h1 - 1), ("R1", u, 1, h1 - 1)], 0.15)
        routes, ends = second_routes(u, units)
        for key, s, hops, _, adds in routes:
            needs = [("F1", u)] + ([("R2", u, adds)] if adds is not None else [])
            put(("S2", u, key), needs, 0.07, [(("R2", u, key), OTHER[first] + str(s), hops, 12288)])
        put(("F2", u), [("R2", u, key) for key in ends], 0.1, [(("O", u), "o" + str(r), 1 + (r == 2) - 2.5 * (r == 0), 12288)])
    depth = {"M": 0, "S1": 1, "F1": 6, "S2": 7, "F2": 12, "X": 50}

    def rank(name):
        level = depth[name[0]]
        if name[0] == "S1":
            level += name[3]
        if name[0] == "X":
            return (-100.0, name[1])
        return (weights[0] * name[1] + weights[1] * level, name[1], -level, name[2:])

    now = start
    order = []
    while tasks:
        best = None
        for name, (needs, _, _) in tasks.items():
            if all(n in done for n in needs):
                at = max(done[n] for n in needs)
                key = (0, 0.0) if at <= now else (1, at)
                if best is None or (key, rank(name)) < best[0]:
                    best = ((key, rank(name)), name, at)
        _, name, at = best
        _, spent, out = tasks.pop(name)
        now = max(now, at) + spent
        done[name] = now
        order.append(name)
        for label, link, hops, size in out or []:
            end = max(links.get(link, 0.0), now) + max(hops, 1) * size / rate
            links[link] = end
            done[label] = end + lat + hop * (hops - 1)
    if detail:
        return order, max(done.values()), done, links
    return order


def attend(len_ref, own_ref, proj_ref, group, core, att):
    lens = [len_ref[j] for j in range(IMGS)]
    ends = [lens[0], lens[0] + lens[1], lens[0] + lens[1] + lens[2]]
    starts = [jnp.int32(0)] + ends
    stops = ends + [ends[2] + lens[3]]
    row = lax.broadcasted_iota(jnp.int32, (ROWS, ROWS), 0)
    col = lax.broadcasted_iota(jnp.int32, (ROWS, ROWS), 1)

    def image(at):
        return sum((at >= e).astype(jnp.int32) for e in ends)

    same = image(row) == image(col)
    scale = HD ** (-0.5)

    def norm(values):
        values = values.astype(F32)
        centred = values - jnp.mean(values, axis=-1, keepdims=True)
        spread = jnp.mean(centred * centred, axis=-1, keepdims=True)
        return (centred * lax.rsqrt(spread + 1e-06)).astype(BF16)

    for h in range(HEADS):
        lanes = slice(h * HD, (h + 1) * HD)
        q = norm(proj_ref[0, :, lanes])
        k = norm(proj_ref[1, :, lanes])
        scores = lax.dot_general(q, k, (((1,), (1,)), ((), ())), preferred_element_type=F32) * scale
        raised = jnp.where(same, jnp.exp(scores), 0.0)
        totals = jnp.sum(raised, axis=-1, keepdims=True)
        weights = (raised / totals).astype(BF16)
        out = jnp.dot(weights, proj_ref[2, :, lanes], preferred_element_type=F32)
        att[:, lanes] = out.astype(BF16)

    stays = jnp.zeros((ROWS, ROWS), jnp.bool_)
    for j in range(IMGS):
        stays = stays | ((row >= starts[j]) & (row < stops[j]) & (own_ref[j] == group))
    picks = [jnp.where((row == col) & stays, 1.0, 0.0).astype(BF16)]
    row64 = lax.broadcasted_iota(jnp.int32, (SPAN, ROWS), 0)
    col64 = lax.broadcasted_iota(jnp.int32, (SPAN, ROWS), 1)
    for target in (group + 1 - 2 * core, group + GROUPS - 1 + 2 * core):
        first = jnp.int32(0)
        stop = jnp.int32(0)
        for j in range(IMGS):
            chosen = own_ref[j] == target % GROUPS
            first = first + jnp.where(chosen, starts[j], 0)
            stop = stop + jnp.where(chosen, stops[j], 0)
        corner = jnp.minimum(first, ROWS - SPAN)
        pick = (col64 == row64 + corner) & (col64 >= first) & (col64 < stop)
        picks.append(jnp.where(pick, 1.0, 0.0).astype(BF16))
    return picks


def order_matrix(y, z, first):
    i = lax.broadcasted_iota(jnp.int32, (HD, HD), 0)
    lane = lax.broadcasted_iota(jnp.int32, (HD, HD), 1)
    block = i >> 2
    if first == "y":
        yd, zd = block >> 3, block
    else:
        yd, zd = block, block >> 2
    yd = (yd + y) & (NY - 1)
    zd = (zd + z) & (NZ - 1)
    d = (yd * NZ + zd) * SHARE + (i & 3)
    return jnp.where(lane == d, 1.0, 0.0).astype(BF16)


def kernel(
    steps, len_ref, own_ref, proj_hbm, cot_ref, att_out, grad_out,
    proj_ref, att, att_all, outb, extra, cotb, gathered, order, partial, sum1_out, sum1_in, sum2, sum2_out, sum2_in, final, result,
    send_sem, recv_sem, local_sem,
):
    y, z, core, x = place()
    other = 1 - core
    chip = y * NZ + z
    group = chip * 2 + core
    after = (chip + 1) % (NY * NZ)
    before = (chip + NY * NZ - 1) % (NY * NZ)
    sibling = device(y, z, other, x)

    def shifted(axis, by, which=None):
        c = core if which is None else which
        if axis == "x":
            return device(y, z, c, x + by % NX)
        if axis == "y":
            return device(y + by % NY, z, c, x)
        return device(y, z + by % NZ, c, x)

    partners = [sibling]
    partners += [shifted("y", by) for by in range(1, NY)]
    partners += [shifted("z", by) for by in range(1, NZ)]
    partners += [shifted("x", by, which) for by in range(1, NX) for which in (0, 1)]
    partners += [(c * 2 + which, x) for c in (after, before) for which in (0, 1)]
    barrier = pltpu.get_barrier_semaphore()
    for p in partners:
        pl.semaphore_signal(barrier, inc=1, device_id=p, device_id_type=MESH)

    loads = []
    for n in range(3):
        copy = pltpu.make_async_copy(proj_hbm.at[n], proj_ref.at[n], local_sem.at[3 + n])
        copy.start()
        loads.append(copy)

    pool = send_sem.shape[0]
    counter = [0]
    sent = []

    def slot_for_send():
        if len(sent) >= pool:
            sent[len(sent) - pool].wait_send()
        return send_sem.at[len(sent) % pool]

    def fresh():
        counter[0] += 1
        return counter[0] - 1

    def message(src, dst, target, n=None):
        copy = pltpu.make_async_remote_copy(
            src_ref=src, dst_ref=dst, send_sem=slot_for_send(), recv_sem=recv_sem.at[fresh() if n is None else n],
            device_id=target, device_id_type=MESH,
        )
        copy.start()
        sent.append(copy)
        return copy

    def landing(dst, n):
        return pltpu.make_async_remote_copy(
            src_ref=dst, dst_ref=dst, send_sem=send_sem.at[0], recv_sem=recv_sem.at[n],
            device_id=sibling, device_id_type=MESH,
        )

    def rows(start, size):
        return pl.ds(pl.multiple_of(start, 64), size)

    mine = ROWS + SPAN
    own_rows = rows(core * mine, mine)
    outer_at = 2 * mine
    cot_pieces = [
        (pl.ds(0, ROWS), rows(core * mine, ROWS)),
        (pl.ds(ROWS, SPAN), rows(other * outer_at + core * ROWS, SPAN)),
        (pl.ds(ROWS + SPAN, SPAN), rows(other * (mine + ROWS) + core * (outer_at + SPAN), SPAN)),
    ]
    cot_here = []
    for n, (src, dst) in enumerate(cot_pieces):
        copy = pltpu.make_async_copy(cot_ref.at[src], cotb.at[dst], local_sem.at[n])
        copy.start()
        cot_here.append(copy)

    for copy in loads:
        copy.wait()
    picks = attend(len_ref, own_ref, proj_ref, group, core, att)
    start = 0
    for pick in picks:
        part = jnp.dot(pick, att[...], preferred_element_type=F32).astype(BF16)
        for h in range(HEADS):
            outb[h // PART, h % PART, start : start + pick.shape[0]] = part[:, h * HD : (h + 1) * HD]
        start += pick.shape[0]
    for h in range(PART):
        gathered[0, h, own_rows] = outb[core, h, 0:mine]
    for n, first in enumerate(("y", "z")):
        order[n] = order_matrix(y, z, first)

    pl.semaphore_wait(barrier, len(partners))

    outer_chip = before * other + after * core
    outer_rows = [pl.ds(outer_at, SPAN), pl.ds(outer_at + SPAN, SPAN)]
    every = pl.ds(0, PART)
    first_heads = pl.ds(0, EARLY)
    last_heads = pl.ds(EARLY, PART - EARLY)

    def crossing(sends, lands):
        base = fresh()
        fresh()
        for which in (0, 1):
            message(*sends(which), base + core)
        return [landing(lands(which), base + which) for which in (0, 1)]

    outer_dst = rows(outer_at + SPAN * other, SPAN)
    outer = crossing(
        lambda which: (
            outb.at[which, every, pl.ds(mine, SPAN)], gathered.at[0, every, outer_dst], (outer_chip * 2 + which, x)
        ),
        lambda which: gathered.at[0, every, outer_rows[1 - which]],
    )
    inner_cp = message(outb.at[other, every, pl.ds(0, mine)], gathered.at[0, every, own_rows], sibling)
    cot_there = [message(cot_ref.at[src], cotb.at[dst], sibling) for src, dst in cot_pieces]

    def send_across(heads):
        return {
            slot: crossing(
                lambda which: (
                    outb.at[which, heads, pl.ds(0, mine)], gathered.at[slot, heads, own_rows],
                    shifted("x", by, which),
                ),
                lambda which: gathered.at[slot, heads, pl.ds(which * mine, mine)],
            )
            for slot, by in ((3, 1), (1, 3))
        }

    across = {0: send_across(first_heads)}
    extra_inner = message(outb.at[core, every, pl.ds(ROWS, SPAN)], extra.at[0], sibling)

    waited = set()
    leaving = []

    def arrived(copy):
        if id(copy) not in waited:
            waited.add(id(copy))
            copy.wait_recv()

    moved = {}

    def forward(label, slot, heads, part):
        by = 1 if slot == 3 else 3
        moved[label] = message(gathered.at[slot, heads, part], gathered.at[2, heads, part], shifted("x", by))

    def write_attended():
        arrived(extra_inner)
        arrived(moved["extra"])
        from_inner = rows(ROWS + SPAN * other, SPAN)
        from_outer = rows(ROWS + SPAN * core, SPAN)
        for h in range(HEADS):
            att_all[0:ROWS, h * HD : (h + 1) * HD] = outb[h // PART, h % PART, 0:ROWS]
        for h in range(PART):
            here = pl.ds(pl.multiple_of(core * HALF + h * HD, HD), HD)
            there = pl.ds(pl.multiple_of(other * HALF + h * HD, HD), HD)
            att_all[from_inner, here] = gathered[0, h, rows(other * mine + ROWS, SPAN)]
            att_all[from_inner, there] = extra[0, h]
            att_all[from_outer, here] = gathered[0, h, rows(outer_at + SPAN * core, SPAN)]
            att_all[from_outer, there] = extra[1, h]
        copy = pltpu.make_async_copy(att_all, att_out, local_sem.at[6])
        copy.start()
        leaving.append(copy)

    def do_move(n):
        if n == 6:
            write_attended()
        elif n == 1:
            for copy in outer:
                arrived(copy)
            both = pl.ds(outer_at, 2 * SPAN)
            moved["po"] = message(gathered.at[0, every, both], gathered.at[3, every, both], shifted("x", 1))
            moved["mo"] = message(gathered.at[0, every, both], gathered.at[1, every, both], shifted("x", 3))
            across[1] = send_across(last_heads)
            arrived(inner_cp)
            theirs = rows(outer_at + SPAN * other, SPAN)
            moved["extra"] = message(gathered.at[0, every, theirs], extra.at[1], sibling)
        elif n == 2:
            arrived(across[0][3][0])
            forward("f0", 3, first_heads, pl.ds(0, mine))
        elif n == 3:
            arrived(across[0][1][1])
            forward("f1", 1, first_heads, pl.ds(mine, mine))
        elif n == 4:
            arrived(moved["po"])
            arrived(moved["mo"])
            forward("f2", 3, every, outer_rows[0])
            forward("f3", 1, every, outer_rows[1])
        elif n == 5:
            arrived(across[1][3][0])
            arrived(across[1][1][1])
            forward("f4", 3, last_heads, pl.ds(0, mine))
            forward("f5", 1, last_heads, pl.ds(mine, mine))

    def do_multiply(u):
        r, h, first, _ = UNITS[u]
        if r == 2:
            for label in ("f0", "f1", "f2", "f3") + (("f4", "f5") if h >= EARLY else ()):
                arrived(moved[label])
        elif r:
            for copy in across[0][r] + (across[1][r] if h >= EARLY else []):
                arrived(copy)
            arrived(moved["po" if r == 3 else "mo"])
        turned = lax.dot_general(
            order["yz".index(first)], gathered[r, h], (((1,), (1,)), ((), ())), preferred_element_type=F32
        ).astype(BF16)
        while cot_here:
            cot_here.pop().wait()
        for copy in cot_there:
            arrived(copy)
        partial[u] = jnp.dot(turned, cotb[...], preferred_element_type=F32)

    received = {}
    shared = {}

    def do_first(u, s, k):
        first = UNITS[u][2]
        n, size = RING[first], BLOCK[first]
        far = n // 2 - k
        rel = far if s == 0 else (n - far) % n
        total = partial[u, rel * size : (rel + 1) * size]
        half = pl.ds(s * FEAT // 2, FEAT // 2) if k == 0 else pl.ds(0, FEAT)
        spot = (u, s, pl.ds(k * size, size), half)
        if k == 0:
            total = total[:, s * FEAT // 2 : (s + 1) * FEAT // 2]
        else:
            received[1, u, s, k - 1].wait_recv()
            before_rows = pl.ds((k - 1) * size, size)
            if k == 1:
                got = sum1_in[u, s, before_rows, s * FEAT // 2 : (s + 1) * FEAT // 2].astype(F32)
                parts = [total[:, : FEAT // 2], total[:, FEAT // 2 :]]
                parts[s] = parts[s] + got
                total = jnp.concatenate(parts, axis=1)
            else:
                total = total + sum1_in[u, s, before_rows].astype(F32)
        sum1_out[spot] = total.astype(BF16)
        last = None
        if k == n // 2 - 1:
            last = shared.setdefault((1, u), -1)
            if last < 0:
                last = shared[1, u] = fresh()
        received[1, u, s, k] = message(
            sum1_out.at[spot], sum1_in.at[spot], shifted(first, 1 if s == 0 else n - 1), last
        )

    def do_turn(u):
        first = UNITS[u][2]
        size, k = BLOCK[first], RING[first] // 2 - 1
        total = partial[u, 0:size]
        landing(sum1_in.at[u, :, pl.ds(k * size, size)], shared[1, u]).wait_recv()
        for s in (0, 1):
            total = total + sum1_in[u, s, pl.ds(k * size, size)].astype(F32)
        for b in range(RING[OTHER[first]]):
            block = total[b * SHARE : (b + 1) * SHARE]
            pieces = [block[:, p * HD : (p + 1) * HD] for p in range(FEAT // HD)]
            sum2[u, b] = jnp.concatenate([p[2 * c : 2 * c + 2] for c in (0, 1) for p in pieces], axis=0)

    def do_second(u, key):
        axis = OTHER[UNITS[u][2]]
        n = RING[axis]
        _, s, hops, rel, adds = next(route for route in second_routes(u, UNITS)[0] if route[0] == key)
        total = sum2[u, rel]
        if adds is not None:
            received[2, u, adds].wait_recv()
            total = total + sum2_in[u, adds].astype(F32)
        sum2_out[u, key] = total.astype(BF16)
        one = None
        if UNITS[u][3]:
            one = shared.setdefault((2, u), -1)
            if one < 0:
                one = shared[2, u] = fresh()
        received[2, u, key] = message(
            sum2_out.at[u, key], sum2_in.at[u, key], shifted(axis, hops if s == 0 else n - hops), one
        )

    arriving = []

    def result_rows(u, source):
        return pl.ds(pl.multiple_of((UNITS[u][1] * NX + source) * (STACK // 2), 8), STACK // 2)

    def do_last(u):
        r = UNITS[u][0]
        total = sum2[u, 0]
        ends = second_routes(u, UNITS)[1]
        if UNITS[u][3]:
            landing(sum2_in.at[u, pl.ds(1, len(ends))], shared[2, u]).wait_recv()
        else:
            for key in ends:
                received[2, u, key].wait_recv()
        for key in ends:
            total = total + sum2_in[u, key].astype(F32)
        final[u, 0] = total[: STACK // 2]
        final[u, 1] = total[STACK // 2 :]
        here = result_rows(u, x)
        if r == 0:
            result[core, here] = final[u, core]
            copy = message(final.at[u, other], result.at[core, here], sibling)
            arriving.append((copy, here))
            return
        n = fresh()
        there = result_rows(u, (x + NX - r) % NX)
        for which in (0, 1):
            message(final.at[u, which], result.at[core, here], shifted("x", r, which), n)
        arriving.append((landing(result.at[:, there], n), there))

    run = {"X": do_move, "M": do_multiply, "S1": do_first, "F1": do_turn, "S2": do_second, "F2": do_last}
    for name in steps:
        run[name[0]](*name[1:])

    for copy, spot in arriving:
        copy.wait_recv()
        pltpu.make_async_copy(result.at[:, spot], grad_out.at[:, spot], local_sem.at[7]).start()
    pltpu.make_async_copy(result, grad_out, local_sem.at[7]).wait()
    for copy in leaving:
        copy.wait()
    assert counter[0] == recv_sem.shape[0]
    for copy in sent[-pool:]:
        copy.wait_send()


def receive_count(units):
    count = 24
    for u, (_, _, first, direct) in enumerate(units):
        count += RING[first] - 1 + (1 if direct else len(second_routes(u, units)[0])) + 1
    return count


def hand_over(attended_in, grads_in, attended_out, grads_out):
    attended_out[...] = attended_in[...]
    grads_out[...] = grads_in[...]


def shards(projected, lengths, owners, cotangent):
    steps = plan_steps(UNITS)
    units = len(UNITS)
    messages = receive_count(UNITS)
    vmem = pl.BlockSpec(memory_space=pltpu.VMEM)
    smem = pl.BlockSpec(memory_space=pltpu.SMEM)
    anywhere = pl.BlockSpec(memory_space=pl.ANY)
    scratch = [
        pltpu.VMEM((3, ROWS, WIDTH), BF16),
        pltpu.VMEM((ROWS, WIDTH), BF16),
        pltpu.VMEM((PACK, WIDTH), BF16),
        pltpu.VMEM((2, PART, PACK, HD), BF16),
        pltpu.VMEM((2, PART, SPAN, HD), BF16),
        pltpu.VMEM((2 * PACK, FEAT), BF16),
        pltpu.VMEM((NX, PART, 2 * PACK, HD), BF16),
        pltpu.VMEM((2, HD, HD), BF16),
        pltpu.VMEM((units, HD, FEAT), F32),
        pltpu.VMEM((units, 2, HD // 2, FEAT), BF16),
        pltpu.VMEM((units, 2, HD // 2, FEAT), BF16),
        pltpu.VMEM((units, NZ, STACK, HD), F32),
        pltpu.VMEM((units, NZ, STACK, HD), BF16),
        pltpu.VMEM((units, NZ, STACK, HD), BF16),
        pltpu.VMEM((units, 2, STACK // 2, HD), F32),
        pltpu.VMEM((2, HEADS * D // HD, HD), F32),
        pltpu.SemaphoreType.DMA((SENDING,)),
        pltpu.SemaphoreType.DMA((messages,)),
        pltpu.SemaphoreType.DMA((8,)),
    ]
    attended, grads = pl.pallas_call(
        functools.partial(kernel, steps),
        out_shape=(
            jax.ShapeDtypeStruct((PACK, WIDTH), BF16),
            jax.ShapeDtypeStruct((2, HEADS * D // HD, HD), F32),
        ),
        in_specs=[smem, smem, anywhere, anywhere],
        out_specs=(anywhere, anywhere),
        scratch_shapes=scratch,
        compiler_params=pltpu.CompilerParams(
            collective_id=0, has_side_effects=True, vmem_limit_bytes=60 * 2**20
        ),
        name="attend_and_reduce",
    )(lengths, owners, projected, cotangent)
    attended, grads = pl.pallas_call(
        hand_over,
        out_shape=(
            jax.ShapeDtypeStruct(attended.shape, BF16),
            jax.ShapeDtypeStruct(grads.shape, F32),
        ),
        in_specs=[vmem, vmem],
        out_specs=(vmem, vmem),
        name="hand_over",
    )(attended, grads)
    grads = grads.reshape(HEADS, D // HD, 2, HD).transpose(0, 2, 1, 3).reshape(HEADS, 2, D)
    return attended, grads


def solution(mesh):
    return jax.shard_map(
        shards,
        mesh=mesh,
        in_specs=(P(None, "dp", "mp"), P("dp"), P("dp"), P("dp", "mp")),
        out_specs=(P("dp", "mp"), P("mp", "dp", None)),
        check_vma=False,
    )
```

```python
import functools

import jax
import jax.numpy as jnp
from jax import lax
from jax.experimental import pallas as pl
from jax.experimental.pallas import tpu as pltpu
from jax.sharding import PartitionSpec as P

MESH = pl.DeviceIdType.MESH
BF16 = jnp.bfloat16
F32 = jnp.float32
NX, NY, NZ = 4, 4, 8
HD = 128
HEADS = 6
PART = HEADS // 2
WIDTH = HEADS * HD
HALF = PART * HD
ROWS = 128
SPAN = 64
PACK = 256
IMGS = 4
GROUPS = 2 * NY * NZ
FEAT = 1536
SHARE = 2 * 2
STACK = SHARE * FEAT // HD
D = 6144
RING = {"y": NY, "z": NZ}
BLOCK = {"y": NZ * SHARE, "z": NY * SHARE}
OTHER = {"y": "z", "z": "y"}

UNITS = [
    (2, 2, "y", 1), (0, 0, "y", 0), (2, 1, "z", 1), (1, 2, "y", 0), (1, 1, "z", 0), (3, 0, "y", 0),
    (0, 2, "z", 1), (3, 1, "y", 0), (2, 0, "z", 1), (0, 1, "y", 0), (1, 0, "z", 0), (3, 2, "y", 1),
]
SENDING = 64


def place():
    dp = lax.axis_index("dp")
    chip = dp // 2
    return chip // NZ, chip % NZ, dp % 2, lax.axis_index("mp")


def device(y, z, core, x):
    return ((y % NY * NZ + z % NZ) * 2 + core, x % NX)


def second_routes(u, units):
    _, _, first, direct = units[u]
    n = RING[OTHER[first]]
    routes = []
    if direct:
        for rel in sorted(range(1, n), key=lambda v: -min(v, n - v)):
            routes.append((rel, 0 if rel <= n // 2 else 1, min(rel, n - rel), rel, None))
        return routes, [route[0] for route in routes]
    for k in range(n // 2):
        for s in (0, 1):
            if k == 0 and s != u % 2:
                continue
            far = n // 2 - k
            adds = s * 4 + k - 1 if k > 1 or (k == 1 and s == u % 2) else None
            routes.append((s * 4 + k, s, 1, far if s == 0 else (n - far) % n, adds))
    return routes, [n // 2 - 1, 4 + n // 2 - 1]


def plan_steps(units, weights=(1.0, 0.0), detail=False):
    start = 9.5
    lat, hop, rate = 2.6, 0.5, 54e3
    done = {"B": start}
    links = {}
    tasks = {}

    def put(name, needs, spent, out=None):
        tasks[name] = (needs, spent, out)

    put(("X", 0), ["B"], 0.3, [
        ("w0", "z0", 1, 49152), ("w1", "z0", 1, 49152), ("p0", "x0", 1, 98304), ("p1", "x0", 1, 98304),
        ("m0", "x1", 1, 98304), ("m1", "x1", 1, 98304),
    ])
    put(("X", 1), ["w0"], 0.5, [("c0", "c", -1.5, 16000)])
    put(("X", 5), ["w1"], 0.5, [("c1", "c", -1.5, 16000)])
    put(("X", 2), ["p0"], 0.1, [("f0", "x0", 1, 98304)])
    put(("X", 3), ["m1"], 0.1, [("f1", "x1", 1, 98304)])
    put(("X", 4), ["f0"], 0.2, None)
    feeds = {0: [], 1: ["m0", "m1"], 3: ["p0", "p1"], 2: ["f0", "f1"]}
    for u, (r, h, first, direct) in enumerate(units):
        h1, h2 = RING[first] // 2, RING[OTHER[first]] // 2
        size = BLOCK[first] * FEAT * 2
        put(("M", u, 0), feeds[r] + ["c0"], 0.25)
        put(("M", u, 1), [("M", u, 0), "c1"], 0.2)
        for k in range(h1):
            for s in (0, 1):
                needs = [("M", u, s)] if k == 0 else [("M", u, 0), ("M", u, 1), ("R1", u, s, k - 1)]
                sent = size // 2 if k == 0 else size
                put(("S1", u, s, k), needs, 0.1, [(("R1", u, s, k), first + str(s), 1, sent)])
        put(("F1", u), [("M", u, 1), ("R1", u, 0, h1 - 1), ("R1", u, 1, h1 - 1)], 0.15)
        routes, ends = second_routes(u, units)
        for key, s, hops, _, adds in routes:
            needs = [("F1", u)] + ([("R2", u, adds)] if adds is not None else [])
            put(("S2", u, key), needs, 0.07, [(("R2", u, key), OTHER[first] + str(s), hops, 12288)])
        put(("F2", u), [("R2", u, key) for key in ends], 0.1, [(("O", u), "o" + str(r), 1 + (r == 2) - 2.5 * (r == 0), 12288)])
    depth = {"M": 0, "S1": 1, "F1": 6, "S2": 7, "F2": 12, "X": 50}

    def rank(name):
        level = depth[name[0]]
        if name[0] == "S1":
            level += name[3]
        if name[0] == "X":
            return (-100.0, name[1])
        return (weights[0] * name[1] + weights[1] * level, name[1], -level, name[2:])

    now = start
    order = []
    while tasks:
        best = None
        for name, (needs, _, _) in tasks.items():
            if all(n in done for n in needs):
                at = max(done[n] for n in needs)
                key = (0, 0.0) if at <= now else (1, at)
                if best is None or (key, rank(name)) < best[0]:
                    best = ((key, rank(name)), name, at)
        _, name, at = best
        _, spent, out = tasks.pop(name)
        now = max(now, at) + 0.5 * spent
        done[name] = now
        order.append(name)
        for label, link, hops, size in out or []:
            end = max(links.get(link, 0.0), now) + max(hops, 1) * size / rate
            links[link] = end
            done[label] = end + lat + hop * (hops - 1)
    if detail:
        return order, max(done.values()), done, links
    return order


def attend(len_ref, own_ref, proj_ref, group, att):
    lens = [len_ref[j] for j in range(IMGS)]
    ends = [lens[0], lens[0] + lens[1], lens[0] + lens[1] + lens[2]]
    starts = [jnp.int32(0)] + ends
    stops = ends + [ends[2] + lens[3]]
    row = lax.broadcasted_iota(jnp.int32, (ROWS, ROWS), 0)
    col = lax.broadcasted_iota(jnp.int32, (ROWS, ROWS), 1)

    def image(at):
        return sum((at >= e).astype(jnp.int32) for e in ends)

    same = image(row) == image(col)
    scale = HD ** (-0.5)

    def norm(values):
        values = values.astype(F32)
        centred = values - jnp.mean(values, axis=-1, keepdims=True)
        spread = jnp.mean(centred * centred, axis=-1, keepdims=True)
        return (centred * lax.rsqrt(spread + 1e-06)).astype(BF16)

    for h in range(HEADS):
        lanes = slice(h * HD, (h + 1) * HD)
        q = norm(proj_ref[0, :, lanes])
        k = norm(proj_ref[1, :, lanes])
        scores = lax.dot_general(q, k, (((1,), (1,)), ((), ())), preferred_element_type=F32) * scale
        raised = jnp.where(same, jnp.exp(scores), 0.0)
        totals = jnp.sum(raised, axis=-1, keepdims=True)
        weights = (raised / totals).astype(BF16)
        out = jnp.dot(weights, proj_ref[2, :, lanes], preferred_element_type=F32)
        att[h // PART, h % PART] = out.astype(BF16)

    row256 = lax.broadcasted_iota(jnp.int32, (ROWS, PACK), 0)
    col256 = lax.broadcasted_iota(jnp.int32, (ROWS, PACK), 1)
    stays = jnp.zeros((ROWS, PACK), jnp.bool_)
    for j in range(IMGS):
        stays = stays | ((row256 >= starts[j]) & (row256 < stops[j]) & (own_ref[j] == group))
    lands = (row256 == col256) & stays
    picks = [jnp.where((row == col) & stays[:, :ROWS], 1.0, 0.0).astype(BF16)]
    row64 = lax.broadcasted_iota(jnp.int32, (SPAN, ROWS), 0)
    col64 = lax.broadcasted_iota(jnp.int32, (SPAN, ROWS), 1)
    for n, step in enumerate((1, GROUPS - 1)):
        target = (group + step) % GROUPS
        first = jnp.int32(0)
        stop = jnp.int32(0)
        for j in range(IMGS):
            chosen = own_ref[j] == target
            first = first + jnp.where(chosen, starts[j], 0)
            stop = stop + jnp.where(chosen, stops[j], 0)
        corner = jnp.minimum(first, ROWS - SPAN)
        pick = (col64 == row64 + corner) & (col64 >= first) & (col64 < stop)
        picks.append(jnp.where(pick, 1.0, 0.0).astype(BF16))
        moves = (row256 >= first) & (row256 < stop)
        lands = lands | ((col256 == row256 - corner + ROWS + SPAN * n) & moves)
    return picks, jnp.where(lands, 1.0, 0.0).astype(BF16)


def order_matrix(y, z, first):
    i = lax.broadcasted_iota(jnp.int32, (HD, HD), 0)
    lane = lax.broadcasted_iota(jnp.int32, (HD, HD), 1)
    block = i >> 2
    if first == "y":
        yd, zd = block >> 3, block
    else:
        yd, zd = block, block >> 2
    yd = (yd + y) & (NY - 1)
    zd = (zd + z) & (NZ - 1)
    d = (yd * NZ + zd) * SHARE + (i & 3)
    return jnp.where(lane == d, 1.0, 0.0).astype(BF16)


def kernel(
    steps, len_ref, own_ref, proj_hbm, cot_ref, att_out, grad_out,
    proj_ref, att, att_all, leave, cot_own, cotb, gathered, order, turned, partial, sum1_out, sum1_in, sum2, sum2_out, sum2_in, final, result,
    send_sem, recv_sem, local_sem,
):
    y, z, core, x = place()
    other = 1 - core
    chip = y * NZ + z
    group = chip * 2 + core
    right = ((group + 1) % GROUPS, x)
    left = ((group + GROUPS - 1) % GROUPS, x)
    sibling = device(y, z, other, x)

    def half_of(c, which):
        return (c // NZ + c % NZ + which) % 2

    part = half_of(chip, core)
    rest = 1 - part

    def shifted(axis, by, which=None):
        if axis == "x":
            return device(y, z, core if which is None else which, x + by % NX)
        c = (core + by) % 2
        if axis == "y":
            return device(y + by % NY, z, c, x)
        return device(y, z + by % NZ, c, x)

    partners = [sibling]
    partners += [shifted("y", by) for by in range(1, NY)]
    partners += [shifted("z", by) for by in range(1, NZ)]
    partners += [shifted("x", by, which) for by in range(1, NX) for which in (0, 1)]
    partners += [left, right]
    barrier = pltpu.get_barrier_semaphore()
    for p in partners:
        pl.semaphore_signal(barrier, inc=1, device_id=p, device_id_type=MESH)

    loads = []
    for n in range(3):
        copy = pltpu.make_async_copy(proj_hbm.at[n], proj_ref.at[n], local_sem.at[3 + n])
        copy.start()
        loads.append(copy)

    pool = send_sem.shape[0]
    counter = [0]
    sent = []

    def slot_for_send():
        if len(sent) >= pool:
            sent[len(sent) - pool].wait_send()
        return send_sem.at[len(sent) % pool]

    def fresh():
        counter[0] += 1
        return counter[0] - 1

    def message(src, dst, target, n=None):
        copy = pltpu.make_async_remote_copy(
            src_ref=src, dst_ref=dst, send_sem=slot_for_send(), recv_sem=recv_sem.at[fresh() if n is None else n],
            device_id=target, device_id_type=MESH,
        )
        copy.start()
        sent.append(copy)
        return copy

    def landing(dst, n):
        return pltpu.make_async_remote_copy(
            src_ref=dst, dst_ref=dst, send_sem=send_sem.at[0], recv_sem=recv_sem.at[n],
            device_id=sibling, device_id_type=MESH,
        )

    def rows(start, size):
        return pl.ds(pl.multiple_of(start, 64), size)

    own_rows = rows(core * ROWS, ROWS)
    cot_here = pltpu.make_async_copy(cot_ref.at[pl.ds(0, ROWS)], cot_own.at[pl.ds(0, ROWS)], local_sem.at[0])
    cot_here.start()

    for copy in loads:
        copy.wait()
    picks, lands = attend(len_ref, own_ref, proj_ref, group, att)
    for h in range(PART):
        gathered[0, h, own_rows] = att[part, h]
    for n, first in enumerate(("y", "z")):
        order[n] = order_matrix(y, z, first)

    pl.semaphore_wait(barrier, len(partners))

    def crossing(sends, lands):
        base = fresh()
        fresh()
        for which in (0, 1):
            message(*sends(which), base + core)
        return [landing(lands(which), base + which) for which in (0, 1)]

    halves = [pl.ds(0, FEAT // 2), pl.ds(FEAT // 2, FEAT // 2)]
    windows = []
    for half in halves:
        first = (pl.ds(ROWS, SPAN), half)
        second = (pl.ds(ROWS + SPAN, SPAN), half)
        windows.append([
            message(cot_ref.at[first], cot_own.at[first], left),
            message(cot_ref.at[second], cot_own.at[second], right),
        ])
    across = {
        slot: crossing(
            lambda which: (
                att.at[half_of(chip, which)], gathered.at[slot, :, own_rows], shifted("x", by, which)
            ),
            lambda which: gathered.at[slot, :, pl.ds(which * ROWS, ROWS)],
        )
        for slot, by in ((3, 1), (1, 3))
    }
    beside = message(att.at[rest], gathered.at[0, :, own_rows], sibling)

    for n, pick in enumerate(picks):
        for h in range(HEADS):
            chosen = jnp.dot(pick, att[h // PART, h % PART], preferred_element_type=F32).astype(BF16)
            if n == 0:
                att_all[0:ROWS, h * HD : (h + 1) * HD] = chosen
            else:
                leave[n - 1, :, h * HD : (h + 1) * HD] = chosen
    came = [
        message(leave.at[0], att_all.at[pl.ds(ROWS, SPAN)], right),
        message(leave.at[1], att_all.at[pl.ds(ROWS + SPAN, SPAN)], left),
    ]

    waited = set()
    leaving = []

    def arrived(copy):
        if id(copy) not in waited:
            waited.add(id(copy))
            copy.wait_recv()

    moved = {}

    def forward(label, slot, heads, part):
        by = 1 if slot == 3 else 3
        moved[label] = message(gathered.at[slot, heads, part], gathered.at[2, heads, part], shifted("x", by))

    def do_move(n):
        if n in (1, 5):
            which = 0 if n == 1 else 1
            if which == 0:
                cot_here.wait()
            for copy in windows[which]:
                copy.wait_recv()
            spot = (own_rows, halves[which])
            cotb[spot] = jnp.dot(lands, cot_own[:, halves[which]], preferred_element_type=F32).astype(BF16)
            moved["c", which] = message(cotb.at[spot], cotb.at[spot], sibling)
        elif n == 2:
            arrived(across[3][0])
            part_rows = pl.ds(0, ROWS)
            moved["f0"] = message(gathered.at[3, :, part_rows], gathered.at[2, :, part_rows], shifted("x", 1))
        elif n == 3:
            arrived(across[1][1])
            part_rows = pl.ds(ROWS, ROWS)
            moved["f1"] = message(gathered.at[1, :, part_rows], gathered.at[2, :, part_rows], shifted("x", 3))
        elif n == 4:
            for copy in came:
                copy.wait_recv()
            copy = pltpu.make_async_copy(att_all, att_out, local_sem.at[6])
            copy.start()
            leaving.append(copy)

    def do_multiply(u, half):
        r, h, first, _ = UNITS[u]
        if half == 0:
            if r == 2:
                arrived(moved["f0"])
                arrived(moved["f1"])
            elif r:
                for copy in across[r]:
                    arrived(copy)
            else:
                arrived(beside)
            turned[u] = lax.dot_general(
                order["yz".index(first)], gathered[r, h], (((1,), (1,)), ((), ())), preferred_element_type=F32
            ).astype(BF16)
        arrived(moved["c", half])
        partial[u, :, halves[half]] = jnp.dot(turned[u], cotb[:, halves[half]], preferred_element_type=F32)

    received = {}
    shared = {}

    def do_first(u, s, k):
        first = UNITS[u][2]
        n, size = RING[first], BLOCK[first]
        far = n // 2 - k
        rel = far if s == 0 else (n - far) % n
        total = partial[u, rel * size : (rel + 1) * size]
        half = pl.ds(s * FEAT // 2, FEAT // 2) if k == 0 else pl.ds(0, FEAT)
        spot = (u, s, pl.ds(k * size, size), half)
        if k == 0:
            total = total[:, s * FEAT // 2 : (s + 1) * FEAT // 2]
        else:
            received[1, u, s, k - 1].wait_recv()
            before_rows = pl.ds((k - 1) * size, size)
            if k == 1:
                got = sum1_in[u, s, before_rows, s * FEAT // 2 : (s + 1) * FEAT // 2].astype(F32)
                parts = [total[:, : FEAT // 2], total[:, FEAT // 2 :]]
                parts[s] = parts[s] + got
                total = jnp.concatenate(parts, axis=1)
            else:
                total = total + sum1_in[u, s, before_rows].astype(F32)
        sum1_out[spot] = total.astype(BF16)
        last = None
        if k == n // 2 - 1:
            last = shared.setdefault((1, u), -1)
            if last < 0:
                last = shared[1, u] = fresh()
        received[1, u, s, k] = message(
            sum1_out.at[spot], sum1_in.at[spot], shifted(first, 1 if s == 0 else n - 1), last
        )

    def do_turn(u):
        first = UNITS[u][2]
        size, k = BLOCK[first], RING[first] // 2 - 1
        total = partial[u, 0:size]
        landing(sum1_in.at[u, :, pl.ds(k * size, size)], shared[1, u]).wait_recv()
        for s in (0, 1):
            total = total + sum1_in[u, s, pl.ds(k * size, size)].astype(F32)
        for b in range(RING[OTHER[first]]):
            block = total[b * SHARE : (b + 1) * SHARE]
            pieces = [block[:, p * HD : (p + 1) * HD] for p in range(FEAT // HD)]
            sum2[u, b] = jnp.concatenate([p[2 * c : 2 * c + 2] for c in (0, 1) for p in pieces], axis=0)

    def do_second(u, key):
        axis = OTHER[UNITS[u][2]]
        n = RING[axis]
        _, s, hops, rel, adds = next(route for route in second_routes(u, UNITS)[0] if route[0] == key)
        total = sum2[u, rel]
        if adds is not None:
            received[2, u, adds].wait_recv()
            total = total + sum2_in[u, adds].astype(F32)
        sum2_out[u, key] = total.astype(BF16)
        one = None
        if UNITS[u][3]:
            one = shared.setdefault((2, u), -1)
            if one < 0:
                one = shared[2, u] = fresh()
        received[2, u, key] = message(
            sum2_out.at[u, key], sum2_in.at[u, key], shifted(axis, hops if s == 0 else n - hops), one
        )

    arriving = []

    def result_rows(u, source):
        return pl.ds(pl.multiple_of((UNITS[u][1] * NX + source) * (STACK // 2), 8), STACK // 2)

    def do_last(u):
        r = UNITS[u][0]
        total = sum2[u, 0]
        ends = second_routes(u, UNITS)[1]
        if UNITS[u][3]:
            landing(sum2_in.at[u, pl.ds(1, len(ends))], shared[2, u]).wait_recv()
        else:
            for key in ends:
                received[2, u, key].wait_recv()
        for key in ends:
            total = total + sum2_in[u, key].astype(F32)
        final[u, 0] = total[: STACK // 2]
        final[u, 1] = total[STACK // 2 :]
        here = result_rows(u, x)
        if r == 0:
            result[part, here] = final[u, core]
            copy = message(final.at[u, other], result.at[part, here], sibling)
            arriving.append((copy, here))
            return
        n = fresh()
        there = result_rows(u, (x + NX - r) % NX)
        for which in (0, 1):
            message(final.at[u, which], result.at[part, here], shifted("x", r, which), n)
        arriving.append((landing(result.at[:, there], n), there))

    run = {"X": do_move, "M": do_multiply, "S1": do_first, "F1": do_turn, "S2": do_second, "F2": do_last}
    for name in steps:
        run[name[0]](*name[1:])

    for copy, spot in arriving:
        copy.wait_recv()
        pltpu.make_async_copy(result.at[:, spot], grad_out.at[:, spot], local_sem.at[7]).start()
    pltpu.make_async_copy(result, grad_out, local_sem.at[7]).wait()
    for copy in leaving:
        copy.wait()
    assert counter[0] == recv_sem.shape[0]
    for copy in sent[-pool:]:
        copy.wait_send()


def receive_count(units):
    count = 15
    for u, (_, _, first, direct) in enumerate(units):
        count += RING[first] - 1 + (1 if direct else len(second_routes(u, units)[0])) + 1
    return count


def hand_over(attended_in, grads_in, attended_out, grads_out):
    attended_out[...] = attended_in[...]
    grads_out[...] = grads_in[...]


def shards(projected, lengths, owners, cotangent):
    steps = plan_steps(UNITS)
    units = len(UNITS)
    messages = receive_count(UNITS)
    vmem = pl.BlockSpec(memory_space=pltpu.VMEM)
    smem = pl.BlockSpec(memory_space=pltpu.SMEM)
    anywhere = pl.BlockSpec(memory_space=pl.ANY)
    scratch = [
        pltpu.VMEM((3, ROWS, WIDTH), BF16),
        pltpu.VMEM((2, PART, ROWS, HD), BF16),
        pltpu.VMEM((PACK, WIDTH), BF16),
        pltpu.VMEM((2, SPAN, WIDTH), BF16),
        pltpu.VMEM((PACK, FEAT), BF16),
        pltpu.VMEM((2 * ROWS, FEAT), BF16),
        pltpu.VMEM((NX, PART, 2 * ROWS, HD), BF16),
        pltpu.VMEM((2, HD, HD), BF16),
        pltpu.VMEM((units, HD, 2 * ROWS), BF16),
        pltpu.VMEM((units, HD, FEAT), F32),
        pltpu.VMEM((units, 2, HD // 2, FEAT), BF16),
        pltpu.VMEM((units, 2, HD // 2, FEAT), BF16),
        pltpu.VMEM((units, NZ, STACK, HD), F32),
        pltpu.VMEM((units, NZ, STACK, HD), BF16),
        pltpu.VMEM((units, NZ, STACK, HD), BF16),
        pltpu.VMEM((units, 2, STACK // 2, HD), F32),
        pltpu.VMEM((2, HEADS * D // HD, HD), F32),
        pltpu.SemaphoreType.DMA((SENDING,)),
        pltpu.SemaphoreType.DMA((messages,)),
        pltpu.SemaphoreType.DMA((8,)),
    ]
    attended, grads = pl.pallas_call(
        functools.partial(kernel, steps),
        out_shape=(
            jax.ShapeDtypeStruct((PACK, WIDTH), BF16),
            jax.ShapeDtypeStruct((2, HEADS * D // HD, HD), F32),
        ),
        in_specs=[smem, smem, anywhere, anywhere],
        out_specs=(anywhere, anywhere),
        scratch_shapes=scratch,
        compiler_params=pltpu.CompilerParams(
            collective_id=0, has_side_effects=True, vmem_limit_bytes=60 * 2**20
        ),
        name="attend_and_reduce",
    )(lengths, owners, projected, cotangent)
    attended, grads = pl.pallas_call(
        hand_over,
        out_shape=(
            jax.ShapeDtypeStruct(attended.shape, BF16),
            jax.ShapeDtypeStruct(grads.shape, F32),
        ),
        in_specs=[vmem, vmem],
        out_specs=(vmem, vmem),
        name="hand_over",
    )(attended, grads)
    grads = grads.reshape(HEADS, D // HD, 2, HD).transpose(0, 2, 1, 3).reshape(HEADS, 2, D)
    return attended, grads


def solution(mesh):
    return jax.shard_map(
        shards,
        mesh=mesh,
        in_specs=(P(None, "dp", "mp"), P("dp"), P("dp"), P("dp", "mp")),
        out_specs=(P("dp", "mp"), P("mp", "dp", None)),
        check_vma=False,
    )
```

```python
import functools

import jax
import jax.numpy as jnp
from jax import lax
from jax.experimental import pallas as pl
from jax.experimental.pallas import tpu as pltpu
from jax.sharding import PartitionSpec as P

MESH = pl.DeviceIdType.MESH
BF16 = jnp.bfloat16
F32 = jnp.float32
NX, NY, NZ = 4, 4, 8
HD = 128
HEADS = 6
PART = HEADS // 2
WIDTH = HEADS * HD
HALF = PART * HD
ROWS = 128
SPAN = 64
PACK = 256
IMGS = 4
GROUPS = 2 * NY * NZ
FEAT = 1536
SHARE = 2 * 2
STACK = SHARE * FEAT // HD
D = 6144
RING = {"y": NY, "z": NZ}
BLOCK = {"y": NZ * SHARE, "z": NY * SHARE}
OTHER = {"y": "z", "z": "y"}

UNITS = [
    (2, 2, "y", 1), (0, 0, "y", 0), (2, 1, "z", 1), (1, 2, "y", 0), (1, 1, "z", 0), (3, 0, "y", 0),
    (0, 2, "z", 1), (3, 1, "y", 0), (2, 0, "z", 1), (0, 1, "y", 0), (1, 0, "z", 0), (3, 2, "y", 1),
]
SENDING = 64


def place():
    dp = lax.axis_index("dp")
    chip = dp // 2
    return chip // NZ, chip % NZ, dp % 2, lax.axis_index("mp")


def device(y, z, core, x):
    return ((y % NY * NZ + z % NZ) * 2 + core, x % NX)


def second_routes(u, units):
    _, _, first, direct = units[u]
    n = RING[OTHER[first]]
    routes = []
    if direct:
        for rel in sorted(range(1, n), key=lambda v: -min(v, n - v)):
            routes.append((rel, 0 if rel <= n // 2 else 1, min(rel, n - rel), rel, None))
        return routes, [route[0] for route in routes]
    for k in range(n // 2):
        for s in (0, 1):
            if k == 0 and s != u % 2:
                continue
            far = n // 2 - k
            adds = s * 4 + k - 1 if k > 1 or (k == 1 and s == u % 2) else None
            routes.append((s * 4 + k, s, 1, far if s == 0 else (n - far) % n, adds))
    return routes, [n // 2 - 1, 4 + n // 2 - 1]


def plan_steps(units, weights=(1.0, 0.0), detail=False):
    start = 9.5
    lat, hop, rate = 2.6, 0.5, 54e3
    done = {"B": start}
    links = {}
    tasks = {}

    def put(name, needs, spent, out=None):
        tasks[name] = (needs, spent, out)

    put(("X", 0), ["B"], 0.3, [
        ("w0", "z0", 1, 49152), ("w1", "z0", 1, 49152), ("p0", "x0", 1, 98304), ("p1", "x0", 1, 98304),
        ("m0", "x1", 1, 98304), ("m1", "x1", 1, 98304),
    ])
    put(("X", 1), ["w0"], 0.5, [("c0", "c", -1.5, 16000)])
    put(("X", 5), ["w1"], 0.5, [("c1", "c", -1.5, 16000)])
    put(("X", 2), ["p0"], 0.1, [("f0", "x0", 1, 98304)])
    put(("X", 3), ["m1"], 0.1, [("f1", "x1", 1, 98304)])
    put(("X", 4), ["f0"], 0.2, None)
    feeds = {0: [], 1: ["m0", "m1"], 3: ["p0", "p1"], 2: ["f0", "f1"]}
    for u, (r, h, first, direct) in enumerate(units):
        h1, h2 = RING[first] // 2, RING[OTHER[first]] // 2
        size = BLOCK[first] * FEAT * 2
        put(("M", u, 0), feeds[r] + ["c0"], 0.25)
        put(("M", u, 1), [("M", u, 0), "c1"], 0.2)
        for k in range(h1):
            for s in (0, 1):
                needs = [("M", u, s)] if k == 0 else [("M", u, 0), ("M", u, 1), ("R1", u, s, k - 1)]
                sent = size // 2 if k == 0 else size
                put(("S1", u, s, k), needs, 0.1, [(("R1", u, s, k), first + str(s), 1, sent)])
        put(("F1", u), [("M", u, 1), ("R1", u, 0, h1 - 1), ("R1", u, 1, h1 - 1)], 0.15)
        routes, ends = second_routes(u, units)
        for key, s, hops, _, adds in routes:
            needs = [("F1", u)] + ([("R2", u, adds)] if adds is not None else [])
            put(("S2", u, key), needs, 0.07, [(("R2", u, key), OTHER[first] + str(s), hops, 12288)])
        put(("F2", u), [("R2", u, key) for key in ends], 0.1, [(("O", u), "o" + str(r), 1 + (r == 2) - 2.5 * (r == 0), 12288)])
    depth = {"M": 0, "S1": 1, "F1": 6, "S2": 7, "F2": 12, "X": 50}

    def rank(name):
        level = depth[name[0]]
        if name[0] == "S1":
            level += name[3]
        if name[0] == "X":
            return (-100.0, name[1])
        return (weights[0] * name[1] + weights[1] * level, name[1], -level, name[2:])

    now = start
    order = []
    while tasks:
        best = None
        for name, (needs, _, _) in tasks.items():
            if all(n in done for n in needs):
                at = max(done[n] for n in needs)
                key = (0, 0.0) if at <= now else (1, at)
                if best is None or (key, rank(name)) < best[0]:
                    best = ((key, rank(name)), name, at)
        _, name, at = best
        _, spent, out = tasks.pop(name)
        now = max(now, at) + 0.5 * spent
        done[name] = now
        order.append(name)
        for label, link, hops, size in out or []:
            end = max(links.get(link, 0.0), now) + max(hops, 1) * size / rate
            links[link] = end
            done[label] = end + lat + hop * (hops - 1)
    if detail:
        return order, max(done.values()), done, links
    return order


def attend(len_ref, own_ref, proj_ref, group, att):
    lens = [len_ref[j] for j in range(IMGS)]
    ends = [lens[0], lens[0] + lens[1], lens[0] + lens[1] + lens[2]]
    starts = [jnp.int32(0)] + ends
    stops = ends + [ends[2] + lens[3]]
    row = lax.broadcasted_iota(jnp.int32, (ROWS, ROWS), 0)
    col = lax.broadcasted_iota(jnp.int32, (ROWS, ROWS), 1)

    def image(at):
        return sum((at >= e).astype(jnp.int32) for e in ends)

    same = image(row) == image(col)
    scale = HD ** (-0.5)

    def norm(values):
        values = values.astype(F32)
        centred = values - jnp.mean(values, axis=-1, keepdims=True)
        spread = jnp.mean(centred * centred, axis=-1, keepdims=True)
        return (centred * lax.rsqrt(spread + 1e-06)).astype(BF16)

    for h in range(HEADS):
        lanes = slice(h * HD, (h + 1) * HD)
        q = norm(proj_ref[0, :, lanes])
        k = norm(proj_ref[1, :, lanes])
        scores = lax.dot_general(q, k, (((1,), (1,)), ((), ())), preferred_element_type=F32) * scale
        raised = jnp.where(same, jnp.exp(scores), 0.0)
        totals = jnp.sum(raised, axis=-1, keepdims=True)
        weights = (raised / totals).astype(BF16)
        out = jnp.dot(weights, proj_ref[2, :, lanes], preferred_element_type=F32)
        att[h // PART, h % PART] = out.astype(BF16)

    row256 = lax.broadcasted_iota(jnp.int32, (ROWS, PACK), 0)
    col256 = lax.broadcasted_iota(jnp.int32, (ROWS, PACK), 1)
    stays = jnp.zeros((ROWS, PACK), jnp.bool_)
    for j in range(IMGS):
        stays = stays | ((row256 >= starts[j]) & (row256 < stops[j]) & (own_ref[j] == group))
    lands = (row256 == col256) & stays
    picks = [jnp.where((row == col) & stays[:, :ROWS], 1.0, 0.0).astype(BF16)]
    row64 = lax.broadcasted_iota(jnp.int32, (SPAN, ROWS), 0)
    col64 = lax.broadcasted_iota(jnp.int32, (SPAN, ROWS), 1)
    for n, step in enumerate((1, GROUPS - 1)):
        target = (group + step) % GROUPS
        first = jnp.int32(0)
        stop = jnp.int32(0)
        for j in range(IMGS):
            chosen = own_ref[j] == target
            first = first + jnp.where(chosen, starts[j], 0)
            stop = stop + jnp.where(chosen, stops[j], 0)
        corner = jnp.minimum(first, ROWS - SPAN)
        pick = (col64 == row64 + corner) & (col64 >= first) & (col64 < stop)
        picks.append(jnp.where(pick, 1.0, 0.0).astype(BF16))
        moves = (row256 >= first) & (row256 < stop)
        lands = lands | ((col256 == row256 - corner + ROWS + SPAN * n) & moves)
    return picks, jnp.where(lands, 1.0, 0.0).astype(BF16)


def order_matrix(y, z, first):
    i = lax.broadcasted_iota(jnp.int32, (HD, HD), 0)
    lane = lax.broadcasted_iota(jnp.int32, (HD, HD), 1)
    block = i >> 2
    if first == "y":
        yd, zd = block >> 3, block
    else:
        yd, zd = block, block >> 2
    yd = (yd + y) & (NY - 1)
    zd = (zd + z) & (NZ - 1)
    d = (yd * NZ + zd) * SHARE + (i & 3)
    return jnp.where(lane == d, 1.0, 0.0).astype(BF16)


def kernel(
    steps, len_hbm, own_hbm, proj_hbm, cot_ref, att_out, grad_out,
    len_ref, own_ref, proj_ref, att, att_all, leave, cot_own, cotb, gathered, order, turned, partial, sum1_out, sum1_in, sum2, sum2_out, sum2_in, final, result,
    send_sem, recv_sem, local_sem,
):
    y, z, core, x = place()
    other = 1 - core
    chip = y * NZ + z
    group = chip * 2 + core
    right = ((group + 1) % GROUPS, x)
    left = ((group + GROUPS - 1) % GROUPS, x)
    sibling = device(y, z, other, x)

    def half_of(c, which):
        return (c // NZ + c % NZ + which) % 2

    part = half_of(chip, core)
    rest = 1 - part

    def shifted(axis, by, which=None):
        if axis == "x":
            return device(y, z, core if which is None else which, x + by % NX)
        c = (core + by) % 2
        if axis == "y":
            return device(y + by % NY, z, c, x)
        return device(y, z + by % NZ, c, x)

    partners = [sibling]
    partners += [shifted("y", by) for by in range(1, NY)]
    partners += [shifted("z", by) for by in range(1, NZ)]
    partners += [shifted("x", by, which) for by in range(1, NX) for which in (0, 1)]
    partners += [left, right]
    barrier = pltpu.get_barrier_semaphore()
    for p in partners:
        pl.semaphore_signal(barrier, inc=1, device_id=p, device_id_type=MESH)

    loads = [
        pltpu.make_async_copy(len_hbm, len_ref, local_sem.at[1]),
        pltpu.make_async_copy(own_hbm, own_ref, local_sem.at[2]),
    ]
    for copy in loads:
        copy.start()
    for n in range(3):
        copy = pltpu.make_async_copy(proj_hbm.at[n], proj_ref.at[n], local_sem.at[3 + n])
        copy.start()
        loads.append(copy)

    pool = send_sem.shape[0]
    counter = [0]
    sent = []

    def slot_for_send():
        if len(sent) >= pool:
            sent[len(sent) - pool].wait_send()
        return send_sem.at[len(sent) % pool]

    def fresh():
        counter[0] += 1
        return counter[0] - 1

    def message(src, dst, target, n=None):
        copy = pltpu.make_async_remote_copy(
            src_ref=src, dst_ref=dst, send_sem=slot_for_send(), recv_sem=recv_sem.at[fresh() if n is None else n],
            device_id=target, device_id_type=MESH,
        )
        copy.start()
        sent.append(copy)
        return copy

    def landing(dst, n):
        return pltpu.make_async_remote_copy(
            src_ref=dst, dst_ref=dst, send_sem=send_sem.at[0], recv_sem=recv_sem.at[n],
            device_id=sibling, device_id_type=MESH,
        )

    def rows(start, size):
        return pl.ds(pl.multiple_of(start, 64), size)

    own_rows = rows(core * ROWS, ROWS)
    cot_here = pltpu.make_async_copy(cot_ref.at[pl.ds(0, ROWS)], cot_own.at[pl.ds(0, ROWS)], local_sem.at[0])
    cot_here.start()

    for copy in loads:
        copy.wait()
    picks, lands = attend(len_ref, own_ref, proj_ref, group, att)
    for h in range(PART):
        gathered[0, h, own_rows] = att[part, h]
    for n, first in enumerate(("y", "z")):
        order[n] = order_matrix(y, z, first)

    pl.semaphore_wait(barrier, len(partners))

    def crossing(sends, lands):
        base = fresh()
        fresh()
        for which in (0, 1):
            message(*sends(which), base + core)
        return [landing(lands(which), base + which) for which in (0, 1)]

    halves = [pl.ds(0, FEAT // 2), pl.ds(FEAT // 2, FEAT // 2)]
    windows = []
    for half in halves:
        first = (pl.ds(ROWS, SPAN), half)
        second = (pl.ds(ROWS + SPAN, SPAN), half)
        windows.append([
            message(cot_ref.at[first], cot_own.at[first], left),
            message(cot_ref.at[second], cot_own.at[second], right),
        ])
    across = {
        slot: crossing(
            lambda which: (
                att.at[half_of(chip, which)], gathered.at[slot, :, own_rows], shifted("x", by, which)
            ),
            lambda which: gathered.at[slot, :, pl.ds(which * ROWS, ROWS)],
        )
        for slot, by in ((3, 1), (1, 3))
    }
    beside = message(att.at[rest], gathered.at[0, :, own_rows], sibling)

    for n, pick in enumerate(picks):
        for h in range(HEADS):
            chosen = jnp.dot(pick, att[h // PART, h % PART], preferred_element_type=F32).astype(BF16)
            if n == 0:
                att_all[0:ROWS, h * HD : (h + 1) * HD] = chosen
            else:
                leave[n - 1, :, h * HD : (h + 1) * HD] = chosen
    came = [
        message(leave.at[0], att_all.at[pl.ds(ROWS, SPAN)], right),
        message(leave.at[1], att_all.at[pl.ds(ROWS + SPAN, SPAN)], left),
    ]

    waited = set()
    leaving = []

    def arrived(copy):
        if id(copy) not in waited:
            waited.add(id(copy))
            copy.wait_recv()

    moved = {}

    def forward(label, slot, heads, part):
        by = 1 if slot == 3 else 3
        moved[label] = message(gathered.at[slot, heads, part], gathered.at[2, heads, part], shifted("x", by))

    def do_move(n):
        if n in (1, 5):
            which = 0 if n == 1 else 1
            if which == 0:
                cot_here.wait()
            for copy in windows[which]:
                copy.wait_recv()
            spot = (own_rows, halves[which])
            cotb[spot] = jnp.dot(lands, cot_own[:, halves[which]], preferred_element_type=F32).astype(BF16)
            moved["c", which] = message(cotb.at[spot], cotb.at[spot], sibling)
        elif n == 2:
            arrived(across[3][0])
            part_rows = pl.ds(0, ROWS)
            moved["f0"] = message(gathered.at[3, :, part_rows], gathered.at[2, :, part_rows], shifted("x", 1))
        elif n == 3:
            arrived(across[1][1])
            part_rows = pl.ds(ROWS, ROWS)
            moved["f1"] = message(gathered.at[1, :, part_rows], gathered.at[2, :, part_rows], shifted("x", 3))
        elif n == 4:
            for copy in came:
                copy.wait_recv()
            copy = pltpu.make_async_copy(att_all, att_out, local_sem.at[6])
            copy.start()
            leaving.append(copy)

    def do_multiply(u, half):
        r, h, first, _ = UNITS[u]
        if half == 0:
            if r == 2:
                arrived(moved["f0"])
                arrived(moved["f1"])
            elif r:
                for copy in across[r]:
                    arrived(copy)
            else:
                arrived(beside)
            turned[u] = lax.dot_general(
                order["yz".index(first)], gathered[r, h], (((1,), (1,)), ((), ())), preferred_element_type=F32
            ).astype(BF16)
        arrived(moved["c", half])
        partial[u, :, halves[half]] = jnp.dot(turned[u], cotb[:, halves[half]], preferred_element_type=F32)

    received = {}
    shared = {}

    def do_first(u, s, k):
        first = UNITS[u][2]
        n, size = RING[first], BLOCK[first]
        far = n // 2 - k
        rel = far if s == 0 else (n - far) % n
        total = partial[u, rel * size : (rel + 1) * size]
        half = pl.ds(s * FEAT // 2, FEAT // 2) if k == 0 else pl.ds(0, FEAT)
        spot = (u, s, pl.ds(k * size, size), half)
        if k == 0:
            total = total[:, s * FEAT // 2 : (s + 1) * FEAT // 2]
        else:
            received[1, u, s, k - 1].wait_recv()
            before_rows = pl.ds((k - 1) * size, size)
            if k == 1:
                got = sum1_in[u, s, before_rows, s * FEAT // 2 : (s + 1) * FEAT // 2].astype(F32)
                parts = [total[:, : FEAT // 2], total[:, FEAT // 2 :]]
                parts[s] = parts[s] + got
                total = jnp.concatenate(parts, axis=1)
            else:
                total = total + sum1_in[u, s, before_rows].astype(F32)
        sum1_out[spot] = total.astype(BF16)
        last = None
        if k == n // 2 - 1:
            last = shared.setdefault((1, u), -1)
            if last < 0:
                last = shared[1, u] = fresh()
        received[1, u, s, k] = message(
            sum1_out.at[spot], sum1_in.at[spot], shifted(first, 1 if s == 0 else n - 1), last
        )

    def do_turn(u):
        first = UNITS[u][2]
        size, k = BLOCK[first], RING[first] // 2 - 1
        total = partial[u, 0:size]
        landing(sum1_in.at[u, :, pl.ds(k * size, size)], shared[1, u]).wait_recv()
        for s in (0, 1):
            total = total + sum1_in[u, s, pl.ds(k * size, size)].astype(F32)
        for b in range(RING[OTHER[first]]):
            block = total[b * SHARE : (b + 1) * SHARE]
            pieces = [block[:, p * HD : (p + 1) * HD] for p in range(FEAT // HD)]
            sum2[u, b] = jnp.concatenate([p[2 * c : 2 * c + 2] for c in (0, 1) for p in pieces], axis=0)

    def do_second(u, key):
        axis = OTHER[UNITS[u][2]]
        n = RING[axis]
        _, s, hops, rel, adds = next(route for route in second_routes(u, UNITS)[0] if route[0] == key)
        total = sum2[u, rel]
        if adds is not None:
            received[2, u, adds].wait_recv()
            total = total + sum2_in[u, adds].astype(F32)
        sum2_out[u, key] = total.astype(BF16)
        one = None
        if UNITS[u][3]:
            one = shared.setdefault((2, u), -1)
            if one < 0:
                one = shared[2, u] = fresh()
        received[2, u, key] = message(
            sum2_out.at[u, key], sum2_in.at[u, key], shifted(axis, hops if s == 0 else n - hops), one
        )

    arriving = []

    def result_rows(u, source):
        return pl.ds(pl.multiple_of((UNITS[u][1] * NX + source) * (STACK // 2), 8), STACK // 2)

    def do_last(u):
        r = UNITS[u][0]
        total = sum2[u, 0]
        ends = second_routes(u, UNITS)[1]
        if UNITS[u][3]:
            landing(sum2_in.at[u, pl.ds(1, len(ends))], shared[2, u]).wait_recv()
        else:
            for key in ends:
                received[2, u, key].wait_recv()
        for key in ends:
            total = total + sum2_in[u, key].astype(F32)
        final[u, 0] = total[: STACK // 2]
        final[u, 1] = total[STACK // 2 :]
        here = result_rows(u, x)
        if r == 0:
            result[part, here] = final[u, core]
            copy = message(final.at[u, other], result.at[part, here], sibling)
            arriving.append((copy, here))
            return
        n = fresh()
        there = result_rows(u, (x + NX - r) % NX)
        for which in (0, 1):
            message(final.at[u, which], result.at[part, here], shifted("x", r, which), n)
        arriving.append((landing(result.at[:, there], n), there))

    run = {"X": do_move, "M": do_multiply, "S1": do_first, "F1": do_turn, "S2": do_second, "F2": do_last}
    for name in steps:
        run[name[0]](*name[1:])

    for copy, spot in arriving:
        copy.wait_recv()
        pltpu.make_async_copy(result.at[:, spot], grad_out.at[:, spot], local_sem.at[7]).start()
    pltpu.make_async_copy(result, grad_out, local_sem.at[7]).wait()
    for copy in leaving:
        copy.wait()
    assert counter[0] == recv_sem.shape[0]
    for copy in sent[-pool:]:
        copy.wait_send()


def receive_count(units):
    count = 15
    for u, (_, _, first, direct) in enumerate(units):
        count += RING[first] - 1 + (1 if direct else len(second_routes(u, units)[0])) + 1
    return count


def hand_over(attended_in, grads_in, attended_out, grads_out):
    attended_out[...] = attended_in[...]
    grads_out[...] = grads_in[...]


def shards(projected, lengths, owners, cotangent):
    steps = plan_steps(UNITS)
    units = len(UNITS)
    messages = receive_count(UNITS)
    vmem = pl.BlockSpec(memory_space=pltpu.VMEM)
    anywhere = pl.BlockSpec(memory_space=pl.ANY)
    scratch = [
        pltpu.SMEM((IMGS,), jnp.int32),
        pltpu.SMEM((IMGS,), jnp.int32),
        pltpu.VMEM((3, ROWS, WIDTH), BF16),
        pltpu.VMEM((2, PART, ROWS, HD), BF16),
        pltpu.VMEM((PACK, WIDTH), BF16),
        pltpu.VMEM((2, SPAN, WIDTH), BF16),
        pltpu.VMEM((PACK, FEAT), BF16),
        pltpu.VMEM((2 * ROWS, FEAT), BF16),
        pltpu.VMEM((NX, PART, 2 * ROWS, HD), BF16),
        pltpu.VMEM((2, HD, HD), BF16),
        pltpu.VMEM((units, HD, 2 * ROWS), BF16),
        pltpu.VMEM((units, HD, FEAT), F32),
        pltpu.VMEM((units, 2, HD // 2, FEAT), BF16),
        pltpu.VMEM((units, 2, HD // 2, FEAT), BF16),
        pltpu.VMEM((units, NZ, STACK, HD), F32),
        pltpu.VMEM((units, NZ, STACK, HD), BF16),
        pltpu.VMEM((units, NZ, STACK, HD), BF16),
        pltpu.VMEM((units, 2, STACK // 2, HD), F32),
        pltpu.VMEM((2, HEADS * D // HD, HD), F32),
        pltpu.SemaphoreType.DMA((SENDING,)),
        pltpu.SemaphoreType.DMA((messages,)),
        pltpu.SemaphoreType.DMA((8,)),
    ]
    attended, grads = pl.pallas_call(
        functools.partial(kernel, steps),
        out_shape=(
            jax.ShapeDtypeStruct((PACK, WIDTH), BF16),
            jax.ShapeDtypeStruct((2, HEADS * D // HD, HD), F32),
        ),
        in_specs=[anywhere] * 4,
        out_specs=(anywhere, anywhere),
        scratch_shapes=scratch,
        compiler_params=pltpu.CompilerParams(
            collective_id=0, has_side_effects=True, vmem_limit_bytes=60 * 2**20
        ),
        name="attend_and_reduce",
    )(lengths, owners, projected, cotangent)
    attended, grads = pl.pallas_call(
        hand_over,
        out_shape=(
            jax.ShapeDtypeStruct(attended.shape, BF16),
            jax.ShapeDtypeStruct(grads.shape, F32),
        ),
        in_specs=[vmem, vmem],
        out_specs=(vmem, vmem),
        name="hand_over",
    )(attended, grads)
    grads = grads.reshape(HEADS, D // HD, 2, HD).transpose(0, 2, 1, 3).reshape(HEADS, 2, D)
    return attended, grads


def solution(mesh):
    return jax.shard_map(
        shards,
        mesh=mesh,
        in_specs=(P(None, "dp", "mp"), P("dp"), P("dp"), P("dp", "mp")),
        out_specs=(P("dp", "mp"), P("mp", "dp", None)),
        check_vma=False,
    )
```
